32 devices in a mesh: dp: 8 (over z, y), fsdp: 4 (over x, core).
Axes of the slice: x: 2, y: 2, z: 4, core: 2. Of those that a mesh axis runs over, the one named last changes fastest.
Arguments:
- inputs: bfloat16 [65536, 384], P(('dp', 'fsdp')), may hold values from -6 to 6
- cotangent: bfloat16 [65536, 384], P(('dp', 'fsdp')), may hold values from -6 to 6
- attn_masks: int32 [1024, 64, 64], P(('dp', 'fsdp')), may hold values 0 or 1
- qkv_weight: float32 [384, 1152], P(('dp', 'fsdp')), may hold values from -0.3125 to 0.3125
- qkv_first: float32 [384, 1152], P(('dp', 'fsdp')), may hold values from -0.0012207031 to 0.0012207031
- qkv_second: float32 [384, 1152], P(('dp', 'fsdp')), may hold values from 2.8257016e-10 to 4.5211226e-09
- proj_weight: float32 [384, 384], P(('dp', 'fsdp')), may hold values from -1.5 to 1.5
- proj_first: float32 [384, 384], P(('dp', 'fsdp')), may hold values from -0.0012207031 to 0.0012207031
- proj_second: float32 [384, 384], P(('dp', 'fsdp')), may hold values from 2.8257016e-10 to 4.5211226e-09
- up_weight: float32 [384, 1536], P(('dp', 'fsdp')), may hold values from -0.3125 to 0.3125
- up_first: float32 [384, 1536], P(('dp', 'fsdp')), may hold values from -0.0012207031 to 0.0012207031
- up_second: float32 [384, 1536], P(('dp', 'fsdp')), may hold values from 2.8257016e-10 to 4.5211226e-09
- down_weight: float32 [1536, 384], P(('dp', 'fsdp')), may hold values from -0.15625 to 0.15625
- down_first: float32 [1536, 384], P(('dp', 'fsdp')), may hold values from -0.0012207031 to 0.0012207031
- down_second: float32 [1536, 384], P(('dp', 'fsdp')), may hold values from 2.8257016e-10 to 4.5211226e-09
- vectors: float32 [3840], P(('dp', 'fsdp')), may hold values from -1.5 to 4.5, as said below
- vector_first: float32 [3840], P(('dp', 'fsdp')), may hold values from -0.0048828125 to 0.0048828125
- vector_second: float32 [3840], P(('dp', 'fsdp')), may hold values from 4.5211226e-09 to 7.233796e-08
Outputs:
- block_out: bfloat16 [65536, 384], P(('dp', 'fsdp'))
- input_grad: float32 [65536, 384], P(('dp', 'fsdp'))
- clip_norm: float32 [], replicated
- qkv_new: float32 [384, 1152], P(('dp', 'fsdp'))
- qkv_first_new: float32 [384, 1152], P(('dp', 'fsdp'))
- qkv_second_new: float32 [384, 1152], P(('dp', 'fsdp'))
- proj_new: float32 [384, 384], P(('dp', 'fsdp'))
- proj_first_new: float32 [384, 384], P(('dp', 'fsdp'))
- proj_second_new: float32 [384, 384], P(('dp', 'fsdp'))
- up_new: float32 [384, 1536], P(('dp', 'fsdp'))
- up_first_new: float32 [384, 1536], P(('dp', 'fsdp'))
- up_second_new: float32 [384, 1536], P(('dp', 'fsdp'))
- down_new: float32 [1536, 384], P(('dp', 'fsdp'))
- down_first_new: float32 [1536, 384], P(('dp', 'fsdp'))
- down_second_new: float32 [1536, 384], P(('dp', 'fsdp'))
- vector_new: float32 [3840], P(('dp', 'fsdp'))
- vector_first_new: float32 [3840], P(('dp', 'fsdp'))
- vector_second_new: float32 [3840], P(('dp', 'fsdp'))
The draws below stay inside these ranges and needn't reach their ends.
Inputs may be any that keep to these rules, and one draw needn't show every extreme that they name: `vectors`: gains and biases of a trained layer.
All inputs are finite; a program needn't handle non-finite values. No bound on the sum of `attn_masks` on one device may be relied on, other than what follows from the above.
Results may differ from the reference program's by a relative error of at most 0.008.
The reference program's roundings to bfloat16 on the way count: a program that leaves them out, or rounds other values in their place, can miss the bound.
Values may be sent and summed in bfloat16 or wider, within the bound.
A program may use at most 128 MiB of HBM per device.

```python
import math
import jax
import jax.numpy as jnp
from jax import lax

D = 384
FF = 1536
HEADS = 6
HD = 64
P_SIZE = 64
STEP = 10
CLOUDS = 1024
TOKENS = 65536
VEC = 3840


def draw_vectors(key, part):
    key = jax.random.fold_in(key, 7)
    subkeys = jax.random.split(key, 3)
    position = jnp.arange(D, dtype=jnp.float32) / (D - 1)
    rising = 3.0 ** position
    jitter = jnp.exp(0.2 * jax.random.normal(subkeys[0], (2, D), jnp.float32))
    shifts = 0.12 * jax.random.normal(subkeys[1], (4, D), jnp.float32)
    up_shift = 0.25 * jax.random.normal(subkeys[2], (FF,), jnp.float32)
    gain_rows = 0.6 * rising * jitter
    joined = jnp.concatenate([gain_rows[0], shifts[0], gain_rows[1], shifts[1], shifts[2], shifts[3], up_shift])
    return jnp.clip(joined, -1.5, 4.5)


def with_ends(values, key, low, largest):
    longest = values.shape.index(max(values.shape))
    spots = []
    for shift in (0, 1):
        where = [jax.random.randint(jax.random.fold_in(key, axis), (), 0, length) for axis, length in enumerate(values.shape)]
        where[longest] = (where[longest] + shift) % values.shape[longest]
        spots.append(tuple(where))
    return values.at[spots[0]].set(low).at[spots[1]].set(largest)


def level_of(stream_key, extent, cuts, smallest, largest):
    def one(dim, shards_of):
        heights = jax.random.uniform(jax.random.fold_in(jax.random.fold_in(stream_key, 6), dim), (shards_of,), jnp.float32, smallest / len(cuts), largest / len(cuts))
        return jnp.repeat(jnp.exp(heights), extent[dim] // shards_of).reshape((-1,) + (1,) * (len(extent) - dim - 1))

    factor_of = one(*cuts[0])
    for cut in cuts[1:]:
        factor_of = factor_of * one(*cut)
    return factor_of


def normal_values(own_key, extent, deviation, most, pieces=(), kind=jnp.bfloat16):
    drawn = deviation * jax.random.normal(own_key, extent, jnp.float32)
    if pieces:
        drawn = drawn * level_of(own_key, extent, pieces, -0.22, 0.18)
    return jnp.clip(drawn, -most, most).astype(kind)


def setup_inputs(seed: int = 0) -> dict:
    arg_keys = jax.random.split(jax.random.key(seed), 19)
    return {
        "inputs": normal_values(arg_keys[0], (TOKENS, D), 1.0, 6.0, ((0, 32),)),
        "cotangent": normal_values(arg_keys[1], (TOKENS, D), 1.0, 6.0, ((0, 32),)),
        "attn_masks": with_ends((jax.random.randint(arg_keys[2], (CLOUDS, P_SIZE, P_SIZE), 0, 4) < 3).astype(jnp.int32), jax.random.fold_in(arg_keys[2], 1), 0, 1),
        "qkv_weight": normal_values(arg_keys[3], (D, 3 * D), D ** -0.5, 0.3125, ((0, 32),), jnp.float32),
        "qkv_first": normal_values(arg_keys[4], (D, 3 * D), (0.11 / (D * (4 * D + 2 * FF)) ** 0.5), 0.0012207031, ((0, 32),), jnp.float32),
        "qkv_second": jnp.clip(jnp.exp(math.log(4.521122587419768e-09) - 2.7725887 * jax.random.uniform(arg_keys[5], (D, 3 * D), jnp.float32) ** level_of(arg_keys[5], (D, 3 * D), ((0, 32),), -0.2, 0.2)), 2.825701617137355e-10, 4.521122587419768e-09),
        "proj_weight": normal_values(arg_keys[6], (D, D), (D // 24) ** -0.5, 1.5, ((0, 32),), jnp.float32),
        "proj_first": normal_values(arg_keys[7], (D, D), (0.11 / (D * (4 * D + 2 * FF)) ** 0.5), 0.0012207031, ((0, 32),), jnp.float32),
        "proj_second": jnp.clip(jnp.exp(math.log(4.521122587419768e-09) - 2.7725887 * jax.random.uniform(arg_keys[8], (D, D), jnp.float32) ** level_of(arg_keys[8], (D, D), ((0, 32),), -0.2, 0.2)), 2.825701617137355e-10, 4.521122587419768e-09),
        "up_weight": normal_values(arg_keys[9], (D, FF), D ** -0.5, 0.3125, ((0, 32),), jnp.float32),
        "up_first": normal_values(arg_keys[10], (D, FF), (0.11 / (D * (4 * D + 2 * FF)) ** 0.5), 0.0012207031, ((0, 32),), jnp.float32),
        "up_second": jnp.clip(jnp.exp(math.log(4.521122587419768e-09) - 2.7725887 * jax.random.uniform(arg_keys[11], (D, FF), jnp.float32) ** level_of(arg_keys[11], (D, FF), ((0, 32),), -0.2, 0.2)), 2.825701617137355e-10, 4.521122587419768e-09),
        "down_weight": normal_values(arg_keys[12], (FF, D), FF ** -0.5, 0.15625, ((0, 32),), jnp.float32),
        "down_first": normal_values(arg_keys[13], (FF, D), (0.11 / (D * (4 * D + 2 * FF)) ** 0.5), 0.0012207031, ((0, 32),), jnp.float32),
        "down_second": jnp.clip(jnp.exp(math.log(4.521122587419768e-09) - 2.7725887 * jax.random.uniform(arg_keys[14], (FF, D), jnp.float32) ** level_of(arg_keys[14], (FF, D), ((0, 32),), -0.2, 0.2)), 2.825701617137355e-10, 4.521122587419768e-09),
        "vectors": draw_vectors(jax.random.fold_in(arg_keys[18], 71), 0),
        "vector_first": normal_values(arg_keys[16], (VEC,), (0.44 / (D * (4 * D + 2 * FF)) ** 0.5), 0.0048828125, ((0, 32),), jnp.float32),
        "vector_second": jnp.clip(jnp.exp(math.log(7.233796139871629e-08) - 2.7725887 * jax.random.uniform(arg_keys[17], (VEC,), jnp.float32) ** level_of(arg_keys[17], (VEC,), ((0, 32),), -0.2, 0.2)), 4.521122587419768e-09, 7.233796139871629e-08),
    }


@jax.custom_vjp
def low(v):
    return lax.optimization_barrier(v.astype(jnp.bfloat16)).astype(jnp.float32)

@jax.custom_vjp
def low_back(v):
    return v

def low_keep(v):
    return (low(v), None)

def low_pass(kept, grad):
    return (grad,)

def back_keep(v):
    return (v, None)

def back_low(kept, grad):
    return (low(grad),)
low.defvjp(low_keep, low_pass)
low_back.defvjp(back_keep, back_low)
norm_eps = 1e-05
beta_first = 0.9
beta_second = 0.999
adam_eps = 1e-08
decay_rate = 0.05
matrix_rates = (0.1, 0.5, 0.1, 0.05)
vector_rate = 1.0
highest = lax.Precision.HIGHEST

def product(left_side, right_side):
    return jnp.dot(left_side, right_side, precision=highest)

def layer_norm(values, scales, offset):
    average = lax.optimization_barrier(jnp.mean(values, axis=-1, keepdims=True))
    centered = values - average
    variance = lax.optimization_barrier(jnp.mean(centered * centered, axis=-1, keepdims=True))
    return centered * lax.rsqrt(variance + norm_eps) * scales + offset

def split_vector(vector):
    return (vector[0:D], vector[D:2 * D], vector[2 * D:3 * D], vector[3 * D:4 * D], vector[4 * D:5 * D], vector[5 * D:6 * D], vector[6 * D:6 * D + FF])

def make_allowed(attn_masks):
    query_pos = lax.broadcasted_iota(jnp.int32, (P_SIZE, P_SIZE), 0)
    key_pos = lax.broadcasted_iota(jnp.int32, (P_SIZE, P_SIZE), 1)
    return (key_pos <= query_pos) & ((attn_masks == 1) | (key_pos == query_pos))

def attend(packed, allowed):
    cloud_count = packed.shape[0]
    shaped = packed.reshape(cloud_count, P_SIZE, 3, HEADS, HD)
    scores = jnp.einsum('cqhd,ckhd->chqk', shaped[:, :, 0], shaped[:, :, 1], precision=highest) * HD ** (-0.5)
    scores = low_back(scores)
    scores = jnp.where(allowed[:, None], scores, -1e+30)
    top_score = lax.optimization_barrier(jnp.max(scores, axis=-1, keepdims=True))
    exponent = jnp.exp(scores - top_score)
    weights = low(exponent / lax.optimization_barrier(jnp.sum(exponent, axis=-1, keepdims=True)))
    mixture = jnp.einsum('chqk,ckhd->cqhd', weights, shaped[:, :, 2], precision=highest)
    return mixture.reshape(cloud_count, P_SIZE, D)

def attend_group(bundle):
    return jax.checkpoint(attend)(bundle[0], bundle[1])

def forward(layer_input, qkv_matrix, proj_matrix, up_matrix, down_matrix, vector, allowed):
    gain_one, bias_one, gain_two, bias_two, proj_bias, down_bias, up_bias = split_vector(vector)
    normed = low(layer_norm(layer_input, gain_one, bias_one))
    packed = low(low_back(product(normed, qkv_matrix)))
    group_size = math.gcd(CLOUDS, 64)
    groups = CLOUDS // group_size
    grouped = packed.reshape(groups, group_size, P_SIZE, 3 * D)
    masked = allowed.reshape(groups, group_size, P_SIZE, P_SIZE)
    mixture = lax.map(attend_group, (grouped, masked)).reshape(TOKENS, D)
    mixture = low(low_back(mixture))
    branch = low_back(product(mixture, proj_matrix) + proj_bias)
    middle = layer_input + branch
    second = low(layer_norm(middle, gain_two, bias_two))
    hidden = low_back(product(second, up_matrix) + up_bias)
    active = low(jax.nn.gelu(hidden, approximate=False))
    branch_two = low_back(product(active, down_matrix) + down_bias)
    return middle + branch_two

def adam_step(master, moment_one, moment_two, gradient, step_rate, decay_coef):
    first_new = beta_first * moment_one + (1.0 - beta_first) * gradient
    second_new = beta_second * moment_two + (1.0 - beta_second) * gradient * gradient
    first_hat = first_new / (1.0 - beta_first ** STEP)
    second_hat = second_new / (1.0 - beta_second ** STEP)
    master_new = master - step_rate * (first_hat / (jnp.sqrt(second_hat) + adam_eps) + decay_coef * master)
    return (master_new, first_new, second_new)

def reference(inputs, cotangent, attn_masks, qkv_weight, qkv_first, qkv_second, proj_weight, proj_first, proj_second, up_weight, up_first, up_second, down_weight, down_first, down_second, vectors, vector_first, vector_second):
    allowed = make_allowed(attn_masks)
    masters = (qkv_weight, proj_weight, up_weight, down_weight, vectors)
    rounded = tuple((matrix.astype(jnp.bfloat16).astype(jnp.float32) for matrix in masters))
    layer_input = inputs.astype(jnp.float32)

    def wrapped(*operands):
        return forward(*operands, allowed)
    result, pullback = jax.vjp(wrapped, layer_input, *rounded)
    gradients = pullback(cotangent.astype(jnp.float32))
    input_grad = gradients[0]
    weight_grads = gradients[1:]
    squares = jnp.float32(0.0)
    for gradient in weight_grads:
        squares = squares + jnp.sum(gradient * gradient)
    clip_norm = jnp.sqrt(squares)
    factor = 1.0 / clip_norm
    qkv_new, qkv_first_new, qkv_second_new = adam_step(qkv_weight, qkv_first, qkv_second, weight_grads[0] * factor, matrix_rates[0], decay_rate)
    proj_new, proj_first_new, proj_second_new = adam_step(proj_weight, proj_first, proj_second, weight_grads[1] * factor, matrix_rates[1], decay_rate)
    up_new, up_first_new, up_second_new = adam_step(up_weight, up_first, up_second, weight_grads[2] * factor, matrix_rates[2], decay_rate)
    down_new, down_first_new, down_second_new = adam_step(down_weight, down_first, down_second, weight_grads[3] * factor, matrix_rates[3], decay_rate)
    vector_new, vector_first_new, vector_second_new = adam_step(vectors, vector_first, vector_second, weight_grads[4] * factor, vector_rate, 0.0)
    return (result.astype(jnp.bfloat16), input_grad, clip_norm, qkv_new, qkv_first_new, qkv_second_new, proj_new, proj_first_new, proj_second_new, up_new, up_first_new, up_second_new, down_new, down_first_new, down_second_new, vector_new, vector_first_new, vector_second_new)
```

```python
import functools
import math

import jax
import jax.numpy as jnp
from jax import lax
from jax.experimental import pallas as pl
from jax.experimental.pallas import tpu as pltpu
from jax.sharding import PartitionSpec as P

D = 384
FF = 1536
HD = 64
STEP = 10
LN_EPS = 1e-05
BETA1 = 0.9
BETA2 = 0.999
ADAM_EPS = 1e-08
DECAY = 0.05
RATES = (0.1, 0.5, 0.1, 0.05)
VECTOR_RATE = 1.0
TB = 256
CH = 256

f32 = jnp.float32
bf16 = jnp.bfloat16
NN = (((1,), (0,)), ((), ()))
NT = (((1,), (1,)), ((), ()))
TN = (((0,), (0,)), ((), ()))
MESH = pl.DeviceIdType.MESH


def dot(a, b, dims=NN):
    return lax.dot_general(a, b, dims, preferred_element_type=f32)


def ln_parts(v):
    centered = v - jnp.mean(v, axis=-1, keepdims=True)
    variance = jnp.mean(centered * centered, axis=-1, keepdims=True)
    return centered, lax.rsqrt(variance + LN_EPS)


def ln_back(grad, xhat, rstd, gain):
    t = grad * gain
    m1 = jnp.mean(t, axis=-1, keepdims=True)
    m2 = jnp.mean(t * xhat, axis=-1, keepdims=True)
    return rstd * (t - m1 - xhat * m2)


def normal_parts(u):
    y = jnp.abs(u) * (2.0**-0.5)
    t = 1.0 / (1.0 + 0.3275911 * y)
    e = jnp.exp(-(y * y))
    tail = t * (
        0.5 * 0.254829592
        + t
        * (
            -0.5 * 0.284496736
            + t * (0.5 * 1.421413741 + t * (-0.5 * 1.453152027 + t * (0.5 * 1.061405429)))
        )
    )
    tail = tail * e
    return jnp.where(u >= 0, 1.0 - tail, tail), e * (1.0 / math.sqrt(2 * math.pi))


def lane_left():
    return lax.broadcasted_iota(jnp.int32, (64, 128), 1) < 64


def two_heads(m, left):
    zero = jnp.zeros_like(m)
    return jnp.concatenate([jnp.where(left, m, zero), jnp.where(left, zero, m)], axis=0)


def diagonal(r, left):
    return jnp.where(left, r[0:64], r[64:128])


def attention_forward(i, mask, qkv, probs, mixed):
    left = lane_left()
    key = lax.broadcasted_iota(jnp.int32, (64, 64), 0)
    query = lax.broadcasted_iota(jnp.int32, (64, 64), 1)
    for c in range(TB // 64):
        cloud = i * (TB // 64) + c
        r = pl.ds(pl.multiple_of(cloud * 64, 64), 64)
        allowed = (key <= query) & ((mask[cloud].T == 1) | (key == query))
        bias = jnp.where(allowed, 0.0, -1e30)
        bias = jnp.concatenate([bias, bias], axis=1)
        for g in range(3):
            q = qkv[r, 128 * g : 128 * g + 128] * jnp.asarray(0.125, bf16)
            k = qkv[r, D + 128 * g : D + 128 * g + 128]
            v = qkv[r, 2 * D + 128 * g : 2 * D + 128 * g + 128]
            s = dot(k, two_heads(q, left), NT) + bias
            e = jnp.exp(s - jnp.max(s, axis=0, keepdims=True))
            p = e * (1.0 / jnp.sum(e, axis=0, keepdims=True))
            probs[r, 128 * g : 128 * g + 128] = p
            o = diagonal(dot(p.astype(bf16), v, TN), left)
            mixed[r, 128 * g : 128 * g + 128] = o.astype(bf16)


def attention_backward(i, qkv, probs, dmix):
    left = lane_left()
    for c in range(TB // 64):
        cloud = i * (TB // 64) + c
        r = pl.ds(pl.multiple_of(cloud * 64, 64), 64)
        for g in range(3):
            sl = slice(128 * g, 128 * g + 128)
            q = qkv[r, 128 * g : 128 * g + 128] * jnp.asarray(0.125, bf16)
            k = qkv[r, D + 128 * g : D + 128 * g + 128]
            v = qkv[r, 2 * D + 128 * g : 2 * D + 128 * g + 128]
            do = two_heads(dmix[r, sl], left)
            p = probs[r, sl]
            dp = dot(v, do, NT)
            ds = (p * (dp - jnp.sum(p * dp, axis=0, keepdims=True))).astype(bf16)
            dv = dot(p.astype(bf16), do)
            dk = dot(ds, two_heads(q, left))
            dq = diagonal(dot(ds, k, TN), left) * 0.125
            qkv[r, 128 * g : 128 * g + 128] = dq.astype(bf16)
            qkv[r, D + 128 * g : D + 128 * g + 128] = dk.astype(bf16)
            qkv[r, 2 * D + 128 * g : 2 * D + 128 * g + 128] = dv.astype(bf16)


def pick_rows(devs, total, shift, step, k, block=None):
    rows = total // devs[2]
    shape = (16 * devs[1], total if block is None else D)
    out = lax.broadcasted_iota(jnp.int32, shape, 0)
    col = lax.broadcasted_iota(jnp.int32, shape, 1)
    if block is not None:
        col = col + D * block
    dev = out >> 4
    i = out - 16 * dev - shift
    ok = (i >= 0) & (i < rows // step) & (col == rows * (dev + devs[0]) + step * i + k)
    return jnp.where(ok, 1.0, 0.0).astype(bf16)


class Layout:
    def __init__(self, n):
        self.n, self.R, self.Rd = n, D // n, FF // n
        R = self.R
        self.fold = 4 * R + 1 <= 16
        groups = [slice(D * k, D * k + D) for k in range(4)]
        if self.fold:
            self.q = [(groups[k], k * R, groups[0]) for k in range(3)]
            self.u = [(groups[k], k * R, groups[0]) for k in range(4)]
            self.p = [(3 * R, 1, 0, groups[0])]
            self.q_sums = [
                (groups[0], [(0, groups[k], k * R, 1, 0) for k in range(3)] + [(1, groups[0], 3 * R, 1, 0)])
            ]
            self.u_sums = [(groups[0], [(groups[k], k * R, 1, 0) for k in range(4)])]
            self.vec_row = 4 * R
            widths = (D, D)
        else:
            self.q = [(slice(0, 3 * D), 0, slice(0, 3 * D))]
            self.u = [(slice(0, FF), 0, slice(0, FF))]
            self.p = [(R, 3, k, groups[k]) for k in range(3)]
            self.q_sums = [
                (groups[k], [(0, groups[k], 0, 1, 0), (1, groups[0], R, 3, k)]) for k in range(3)
            ]
            self.u_sums = [(slice(0, FF), [(slice(0, FF), 0, 1, 0)])]
            self.vec_row = R
            widths = (3 * D, FF)
        tall = self.Rd if self.Rd % 16 == 0 else 16
        self.wide = ((16, widths[0]), (16, widths[1]), (tall, D))

    def p_place(self, i):
        if self.fold:
            return 3 * self.R + i, slice(0, D)
        return self.R + i // 3, slice(D * (i % 3), D * (i % 3) + D)


def layer_kernel(
    dims,
    x_hbm, dy_hbm, mask_hbm, wq_own, wp_own, wu_own, wd_own, vec_own,
    out_hbm, ig_hbm, gq_out, gu_out, gd_out, small_out,
    x, dy, mask, a, qkv, probs, mixed, h1, z_t, du_t,
    gq, gu, gd, wq, wp, wu, wd, vec, bu, vgrid, stage_q, stage_u, stage_d,
    acc_q, acc_p, acc_u, acc_d, dvec, dbu,
    r1q, r1u, r1d, r2q, r2u, r2d, r3q, r3u, r3d,
    small, s1, s2, s3,
    local_sem, ag_send, ag_recv, rs_send, rs_recv, ar_send, ar_recv,
):
    Z, Y, X = dims
    n = Z * Y * X * 2
    lay = Layout(n)
    R, Rd = lay.R, lay.Rd
    T = x.shape[0]
    V = vec_own.shape[1]
    steps = T // TB
    dp = lax.axis_index("dp")
    fs = lax.axis_index("fsdp")
    z, y = dp // Y, dp % Y
    xx, core = fs // 2, fs % 2

    loads = [
        pltpu.make_async_copy(x_hbm, x, local_sem.at[0]),
        pltpu.make_async_copy(mask_hbm, mask, local_sem.at[1]),
        pltpu.make_async_copy(dy_hbm, dy, local_sem.at[2]),
    ]
    for c in loads:
        c.start()

    z_peers = [(k, lax.rem(z + k, Z)) for k in range(1, Z)]
    p_peers = [
        (k, lax.rem(y + k // X, Y), lax.rem(xx + k % X, X)) for k in range(1, X * Y)
    ]
    z_ids = [(zz * Y + y, fs) for _, zz in z_peers]
    p_ids = [(z * Y + yy, pxx * 2 + core) for _, yy, pxx in p_peers]
    c_id = (dp, fs + 1 - 2 * core)
    P1, P2 = len(z_ids), len(p_ids)

    barrier = pltpu.get_barrier_semaphore()
    for dev in z_ids + p_ids + [c_id]:
        pl.semaphore_signal(barrier, inc=1, device_id=dev, device_id_type=MESH)

    stage_q[...] = jnp.zeros_like(stage_q)
    stage_u[...] = jnp.zeros_like(stage_u)
    stage_d[...] = jnp.zeros_like(stage_d)
    for cols, shift, at in lay.q:
        stage_q[shift : shift + R, at] = wq_own[:, cols]
    for i in range(R):
        shift, at = lay.p_place(i)
        stage_q[shift : shift + 1, at] = wp_own[i : i + 1]
    for cols, shift, at in lay.u:
        stage_u[shift : shift + R, at] = wu_own[:, cols]
    stage_u[lay.vec_row : lay.vec_row + 1, 0:V] = vec_own[...]
    stage_d[0:Rd] = wd_own[...]
    gq[z, y, xx, core] = stage_q[...].astype(bf16)
    gu[z, y, xx, core] = stage_u[...].astype(bf16)
    gd[z, y, xx, core] = stage_d[...].astype(bf16)

    pl.semaphore_wait(barrier, P1 + P2 + 1)

    def remote(src, dst, send, recv, dev):
        return pltpu.make_async_remote_copy(
            src_ref=src, dst_ref=dst, send_sem=send, recv_sem=recv, device_id=dev, device_id_type=MESH
        )

    def gather(ch, g, stage):
        if stage == 0:
            return [
                remote(g.at[z, y, xx, core], g.at[z, y, xx, core], ag_send.at[ch, j], ag_recv.at[ch, j], z_ids[j])
                for j in range(P1)
            ]
        if stage == 1:
            return [
                remote(g.at[:, y, xx, core], g.at[:, y, xx, core], ag_send.at[ch, P1 + j], ag_recv.at[ch, P1 + j], p_ids[j])
                for j in range(P2)
            ]
        return [
            remote(g.at[:, :, :, core], g.at[:, :, :, core], ag_send.at[ch, P1 + P2], ag_recv.at[ch, P1 + P2], c_id)
        ]

    bufs = (gq, gu, gd)
    for ch in range(3):
        for c in gather(ch, bufs[ch], 0):
            c.start()
    for stage in (1, 2, 3):
        for ch in range(3):
            for c in gather(ch, bufs[ch], stage - 1):
                c.wait()
            if stage < 3:
                for c in gather(ch, bufs[ch], stage):
                    c.start()

    per_z = 2 * X * Y
    z_group = max(1, min(Z, 32 // per_z))
    groups = [(k, k + z_group, (k * per_z, z_group * per_z, n)) for k in range(0, Z, z_group)]

    def unpack(g, terms, into, cols, via):
        def part(z0, devs):
            flat = g[pl.ds(z0, z_group)].reshape(16 * z_group * per_z, g.shape[-1])
            return sum(
                dot(pick_rows(devs, rows, shift, step, k, *rest), flat[:, at], TN)
                for rows, shift, step, k, at, *rest in terms
            )

        if len(groups) == 1:
            into[:, cols] = part(0, groups[0][2]).astype(bf16)
            return
        via[:, cols] = jnp.zeros((via.shape[0], cols.stop - cols.start), f32)

        @pl.loop(0, len(groups))
        def _(k):
            d0 = k * z_group * per_z
            via[:, cols] += part(k * z_group, (d0, z_group * per_z, n))

        into[:, cols] = via[:, cols].astype(bf16)

    every = slice(0, D)
    for cols, shift, at in lay.q:
        unpack(gq, [(D, shift, 1, 0, at)], wq, cols, acc_q)
    for cols, shift, at in lay.u:
        unpack(gu, [(D, shift, 1, 0, at)], wu, cols, acc_u)
    unpack(gq, [(D,) + p for p in lay.p], wp, every, acc_p)
    if Rd % 16 == 0:
        wd[...] = gd[...].reshape(FF, D)
    else:
        for k in range(FF // D):
            unpack(gd, [(FF, 0, 1, 0, every, k)], wd.at[D * k : D * k + D], every, acc_p)
    for z0, z1, devs in groups:
        first, count, _ = devs
        row = lax.broadcasted_iota(jnp.int32, (count, 16 * count), 0)
        col = lax.broadcasted_iota(jnp.int32, (count, 16 * count), 1)
        pick_vec = jnp.where(col == 16 * row + lay.vec_row, 1.0, 0.0).astype(bf16)
        vgrid[first : first + count] = dot(pick_vec, gu[z0:z1, :, :, :, :, 0:128].reshape(16 * count, 128))
    for d in range(n):
        start, stop = V * d, V * d + V
        while start < stop:
            r0, l0 = start // D, start % D
            size = min(stop - start, D - l0)
            o = start - V * d
            vec[r0 : r0 + 1, l0 : l0 + size] = vgrid[d : d + 1, o : o + size]
            start += size
    for k in range(FF // D):
        bu[:, D * k : D * k + D] = vec[6 + k : 7 + k]

    for r in (acc_q, acc_p, acc_u, acc_d, dvec, dbu):
        r[...] = jnp.zeros_like(r)
    for c in loads:
        c.wait()

    @pl.loop(0, steps)
    def _(i):
        rows = pl.ds(pl.multiple_of(i * TB, TB), TB)
        xv = x[rows, :].astype(f32)
        centered, rstd = ln_parts(xv)
        av = (centered * rstd * vec[0:1] + vec[1:2]).astype(bf16)
        a[rows, :] = av
        qkv[rows, :] = dot(av, wq[...]).astype(bf16)
        attention_forward(i, mask, qkv, probs, mixed)
        h1[rows, :] = xv + (dot(mixed[rows, :], wp[...]) + vec[4:5])

    @pl.loop(0, steps)
    def _(i):
        rows = pl.ds(pl.multiple_of(i * TB, TB), TB)
        h = h1[rows, :]
        centered, rstd = ln_parts(h)
        xhat = centered * rstd
        c = (xhat * vec[2:3] + vec[3:4]).astype(bf16)
        dyv = dy[rows, :]
        for k in range(FF // CH):
            ns = slice(k * CH, (k + 1) * CH)
            u = dot(c, wu[:, ns]) + bu[:, ns]
            dz = dot(dyv, wd[ns, :], NT)
            cdf, density = normal_parts(u)
            zv = (u * cdf).astype(bf16)
            du = (dz * (cdf + u * density)).astype(bf16)
            z_t[:, ns] = zv
            du_t[:, ns] = du
            acc_d[:, ns] += dot(dyv, zv, TN)
            acc_u[:, ns] += dot(c, du, TN)
            dbu[:, ns] += jnp.sum(du.astype(f32), axis=0, keepdims=True)
        dy[rows, :] = (h + (dot(z_t[...], wd[...]) + vec[5:6])).astype(bf16)
        dc = dot(du_t[...], wu[...], NT)
        dyf = dyv.astype(f32)
        dvec[2:3] += jnp.sum(dc * xhat, axis=0, keepdims=True)
        dvec[3:4] += jnp.sum(dc, axis=0, keepdims=True)
        dvec[5:6] += jnp.sum(dyf, axis=0, keepdims=True)
        dh1 = dyf + ln_back(dc, xhat, rstd, vec[2:3])
        h1[rows, :] = dh1
        dr = dh1.astype(bf16)
        dvec[4:5] += jnp.sum(dr.astype(f32), axis=0, keepdims=True)
        acc_p[...] += dot(mixed[rows, :], dr, TN)
        mixed[rows, :] = dot(dr, wp[...], NT).astype(bf16)

    put_out = pltpu.make_async_copy(dy, out_hbm, local_sem.at[3])
    put_out.start()

    @pl.loop(0, steps)
    def _(i):
        rows = pl.ds(pl.multiple_of(i * TB, TB), TB)
        attention_backward(i, qkv, probs, mixed)
        acc_q[...] += dot(a[rows, :], qkv[rows, :], TN)

    @pl.loop(0, steps)
    def _(i):
        rows = pl.ds(pl.multiple_of(i * TB, TB), TB)
        da = dot(qkv[rows, :], wq[...], NT)
        centered, rstd = ln_parts(x[rows, :].astype(f32))
        xhat = centered * rstd
        dvec[0:1] += jnp.sum(da * xhat, axis=0, keepdims=True)
        dvec[1:2] += jnp.sum(da, axis=0, keepdims=True)
        h1[rows, :] = h1[rows, :] + ln_back(da, xhat, rstd, vec[0:1])

    put_ig = pltpu.make_async_copy(h1, ig_hbm, local_sem.at[4])
    put_ig.start()

    def pack(g, at, terms):
        def one(k):
            devs = (k * z_group * per_z, z_group * per_z, n)
            total = sum(
                dot(pick_rows(devs, rows, shift, step, j), source[:, cols].astype(bf16))
                for source, cols, rows, shift, step, j in terms
            )
            shape = (z_group,) + g.shape[1:5] + (total.shape[1],)
            g[pl.ds(k * z_group, z_group), :, :, :, :, at] = total.astype(bf16).reshape(shape)

        if len(groups) == 1:
            one(0)
        else:
            pl.loop(0, len(groups))(one)

    for at, terms in lay.q_sums:
        pack(gq, at, [((acc_q, acc_p)[t[0]], t[1], D) + t[2:] for t in terms])
    for at, terms in lay.u_sums:
        pack(gu, at, [(acc_u, t[0], D) + t[1:] for t in terms])
    if Rd % 16 == 0:
        gd[...] = acc_d[...].astype(bf16).T.reshape(gd.shape)
    else:
        wd[...] = acc_d[...].astype(bf16).T
        pack(gd, slice(0, D), [(wd, slice(0, D), FF, 0, 1, 0)])

    r1 = (r1q, r1u, r1d)
    r2 = (r2q, r2u, r2d)
    r3 = (r3q, r3u, r3d)
    outs = (gq_out, gu_out, gd_out)

    def scatter(ch, stage):
        g = bufs[ch]
        if stage == 0:
            return [remote(g.at[:, :, :, 1 - core], r1[ch], rs_send.at[ch, P1 + P2], rs_recv.at[ch, P1 + P2], c_id)]
        if stage == 1:
            return [
                remote(g.at[:, p_peers[j][1], p_peers[j][2], core], r2[ch].at[j], rs_send.at[ch, P1 + j], rs_recv.at[ch, P1 + j], p_ids[j])
                for j in range(P2)
            ]
        return [
            remote(g.at[z_peers[j][1], y, xx, core], r3[ch].at[j], rs_send.at[ch, j], rs_recv.at[ch, j], z_ids[j])
            for j in range(P1)
        ]

    def add(ch, stage):
        g = bufs[ch]
        if stage == 0:
            for zz in range(Z):
                for yy in range(Y):
                    for cx in range(X):
                        t = g[zz, yy, cx, core].astype(f32) + r1[ch][zz, yy, cx].astype(f32)
                        g[zz, yy, cx, core] = t.astype(bf16)
        elif stage == 1:
            for zz in range(Z):
                t = g[zz, y, xx, core].astype(f32)
                for j in range(P2):
                    t = t + r2[ch][j, zz].astype(f32)
                g[zz, y, xx, core] = t.astype(bf16)
        else:
            t = g[z, y, xx, core].astype(f32)
            for j in range(P1):
                t = t + r3[ch][j].astype(f32)
            outs[ch][...] = t

    for ch in range(3):
        for c in scatter(ch, 0):
            c.start()
    for stage in range(3):
        for ch in range(3):
            for c in scatter(ch, stage):
                c.wait()
            add(ch, stage)
            if stage < 2:
                for c in scatter(ch, stage + 1):
                    c.start()

    squares = jnp.zeros((1, 1), f32)
    for ch in range(3):
        t = outs[ch][...]
        squares = squares + jnp.sum(jnp.sum(t * t, axis=0, keepdims=True), axis=1, keepdims=True)
    small[0] = jnp.zeros((16, D), f32)
    small[0, 0:6] = dvec[0:6]
    for k in range(FF // D):
        small[0, 6 + k : 7 + k] = dbu[:, D * k : D * k + D]
    small[0, 10:11] = jnp.broadcast_to(squares, (1, D))

    def spread(stage):
        if stage == 0:
            return [remote(small.at[0], s1.at[j], ar_send.at[j], ar_recv.at[j], z_ids[j]) for j in range(P1)]
        if stage == 1:
            return [remote(small.at[1], s2.at[j], ar_send.at[P1 + j], ar_recv.at[P1 + j], p_ids[j]) for j in range(P2)]
        return [remote(small.at[2], s3.at[0], ar_send.at[P1 + P2], ar_recv.at[P1 + P2], c_id)]

    received = (s1, s2, s3)
    for stage in range(3):
        copies = spread(stage)
        for c in copies:
            c.start()
        for c in copies:
            c.wait()
        t = small[stage]
        for j in range(len(copies)):
            t = t + received[stage][j]
        if stage < 2:
            small[stage + 1] = t
        else:
            small_out[...] = t
    put_out.wait()
    put_ig.wait()


def layer_call(dims, x, dy, masks, wq, wp, wu, wd, vec):
    Z, Y, X = dims
    n = Z * Y * X * 2
    T = x.shape[0]
    S = jax.ShapeDtypeStruct
    V = pltpu.VMEM
    vm = pl.BlockSpec(memory_space=pltpu.VMEM)
    hbm = pl.BlockSpec(memory_space=pl.ANY)
    peers = (Z - 1) + (X * Y - 1) + 1
    wide = Layout(n).wide
    scratch = [
        V((T, D), bf16), V((T, D), bf16), V(masks.shape, jnp.int32),
        V((T, D), bf16), V((T, 3 * D), bf16), V((T, D), f32), V((T, D), bf16), V((T, D), f32),
        V((TB, FF), bf16), V((TB, FF), bf16),
    ]
    scratch += [V((Z, Y, X, 2) + w, bf16) for w in wide]
    scratch += [V((D, 3 * D), bf16), V((D, D), bf16), V((D, FF), bf16), V((FF, D), bf16)]
    scratch += [V((16, D), f32), V((1, FF), f32), V((n, 128), f32)]
    scratch += [V(w, f32) for w in wide]
    scratch += [V((D, 3 * D), f32), V((D, D), f32), V((D, FF), f32), V((D, FF), f32), V((8, D), f32), V((1, FF), f32)]
    scratch += [V((Z, Y, X) + w, bf16) for w in wide]
    scratch += [V((X * Y - 1, Z) + w, bf16) for w in wide]
    scratch += [V((Z - 1,) + w, bf16) for w in wide]
    scratch += [V((3, 16, D), f32), V((Z - 1, 16, D), f32), V((X * Y - 1, 16, D), f32), V((1, 16, D), f32)]
    dma = pltpu.SemaphoreType.DMA
    scratch += [dma((5,)), dma((3, peers)), dma((3, peers)), dma((3, peers)), dma((3, peers)), dma((peers,)), dma((peers,))]
    return pl.pallas_call(
        functools.partial(layer_kernel, dims),
        out_shape=[S((T, D), bf16), S((T, D), f32)] + [S(w, f32) for w in wide] + [S((16, D), f32)],
        in_specs=[hbm] * 3 + [vm] * 5,
        out_specs=[hbm] * 2 + [vm] * 4,
        scratch_shapes=scratch,
        compiler_params=pltpu.CompilerParams(
            collective_id=0, has_side_effects=True, vmem_limit_bytes=60 * 1024 * 1024
        ),
        name="layer",
    )(x, dy, masks, wq, wp, wu, wd, vec)


def adam_step(w, m, r, g, rate, decay):
    m_new = BETA1 * m + (1.0 - BETA1) * g
    r_new = BETA2 * r + (1.0 - BETA2) * g * g
    m_hat = m_new / (1.0 - BETA1**STEP)
    r_hat = r_new / (1.0 - BETA2**STEP)
    return w - rate * (m_hat / (jnp.sqrt(r_hat) + ADAM_EPS) + decay * w), m_new, r_new


def adam_kernel(n, *refs):
    small, gq, gu, gd = refs[0:4]
    state = refs[4:19]
    out_in, ig_in = refs[19:21]
    out_ref, ig_ref, norm = refs[21:24]
    new = refs[24:39]
    sem = refs[39]
    out_v, ig_v = refs[40:42]
    lay = Layout(n)
    R, Rd, V = lay.R, lay.Rd, state[12].shape[1]
    T = out_v.shape[0]
    parts = [pl.ds(k * (T // 4), T // 4) for k in range(4)]
    loads = [pltpu.make_async_copy(out_in.at[r], out_v.at[r], sem.at[k]) for k, r in enumerate(parts)]
    loads += [pltpu.make_async_copy(ig_in.at[r], ig_v.at[r], sem.at[4 + k]) for k, r in enumerate(parts)]
    stores = [pltpu.make_async_copy(out_v.at[r], out_ref.at[r], sem.at[8 + k]) for k, r in enumerate(parts)]
    stores += [pltpu.make_async_copy(ig_v.at[r], ig_ref.at[r], sem.at[12 + k]) for k, r in enumerate(parts)]
    for c in loads:
        c.start()
    for c, d in zip(loads, stores):
        c.wait()
        d.start()
    vecs = small[0:10]
    squares = jnp.sum(jnp.sum(vecs * vecs, axis=0, keepdims=True), axis=1, keepdims=True) + small[10:11, 0:1]
    clip = jnp.sqrt(squares)
    norm[...] = clip
    factor = 1.0 / clip

    def step(k, rows, cols, g, rate, decay):
        w, m, r = (ref[rows, cols] for ref in state[3 * k : 3 * k + 3])
        for ref, value in zip(new[3 * k : 3 * k + 3], adam_step(w, m, r, g * factor, rate, decay)):
            ref[rows, cols] = value

    every = slice(0, D)
    for cols, shift, at in lay.q:
        step(0, slice(0, R), cols, gq[shift : shift + R, at], RATES[0], DECAY)
    for i in range(R):
        shift, at = lay.p_place(i)
        step(1, slice(i, i + 1), every, gq[shift : shift + 1, at], RATES[1], DECAY)
    for cols, shift, at in lay.u:
        step(2, slice(0, R), cols, gu[shift : shift + R, at], RATES[2], DECAY)
    step(3, slice(0, Rd), every, gd[0:Rd], RATES[3], DECAY)
    me = lax.axis_index("dp") * (n // lax.axis_size("dp")) + lax.axis_index("fsdp")
    start = me * V
    row, lane = start // D, lax.rem(start, D)
    two = jnp.concatenate([small[pl.ds(row, 1), :], small[pl.ds(row + 1, 1), :]], axis=1)
    two = pltpu.roll(jnp.broadcast_to(two, (8, 2 * D)), 2 * D - lane, 1)
    step(4, slice(0, 1), slice(0, V), two[0:1, 0:V], VECTOR_RATE, 0.0)
    for c in stores:
        c.wait()


def adam_call(n, small, gq, gu, gd, state, out, ig):
    vm = pl.BlockSpec(memory_space=pltpu.VMEM)
    hbm = pl.BlockSpec(memory_space=pl.ANY)
    S = jax.ShapeDtypeStruct
    return pl.pallas_call(
        functools.partial(adam_kernel, n),
        out_shape=[S(out.shape, out.dtype), S(ig.shape, ig.dtype), S((1, 1), f32)] + [S(s.shape, f32) for s in state],
        in_specs=[vm] * 19 + [hbm] * 2,
        out_specs=[hbm] * 2 + [vm] * 16,
        scratch_shapes=[pltpu.SemaphoreType.DMA((16,)), pltpu.VMEM(out.shape, out.dtype), pltpu.VMEM(ig.shape, ig.dtype)],
        name="adam",
    )(small, gq, gu, gd, *state, out, ig)


def solution(mesh):
    n_dp, n_fs = mesh.shape["dp"], mesh.shape["fsdp"]
    X = n_fs // 2
    Y = X if n_dp % X == 0 else 1
    dims = (n_dp // Y, Y, X)
    n = n_dp * n_fs

    def per_device(x, dy, masks, *state):
        state = list(state)
        flat = [s.shape for s in state[12:15]]
        state[12:15] = [s.reshape(1, -1) for s in state[12:15]]
        out, ig, gq, gu, gd, small = layer_call(
            dims, x, dy, masks, state[0], state[3], state[6], state[9], state[12]
        )
        res = adam_call(n, small, gq, gu, gd, state, out, ig)
        new = list(res[3:])
        new[12:15] = [v.reshape(f) for v, f in zip(new[12:15], flat)]
        return (res[0], res[1], res[2].reshape(()), *new)

    rows = P(("dp", "fsdp"), None)
    line = P(("dp", "fsdp"))
    placed = (rows, rows, P(("dp", "fsdp"), None, None)) + (rows,) * 12 + (line,) * 3
    given = (rows, rows, P()) + (rows,) * 12 + (line,) * 3
    return jax.shard_map(per_device, mesh=mesh, in_specs=placed, out_specs=given, check_vma=False)
```

```python
import functools
import math

import jax
import jax.numpy as jnp
from jax import lax
from jax.experimental import pallas as pl
from jax.experimental.pallas import tpu as pltpu
from jax.sharding import PartitionSpec as P

D = 384
FF = 1536
HD = 64
STEP = 10
NORM_EPS = 1e-05
BETA1 = 0.9
BETA2 = 0.999
ADAM_EPS = 1e-08
DECAY = 0.05
RATES = (0.1, 0.5, 0.1, 0.05)
VECTOR_RATE = 1.0
TB = 512
TA = 1024
CH = 512

f32 = jnp.float32
bf16 = jnp.bfloat16
NN = (((1,), (0,)), ((), ()))
NT = (((1,), (1,)), ((), ()))
TN = (((0,), (0,)), ((), ()))
MESH = pl.DeviceIdType.MESH


def dot(a, b, dims=NN):
    return lax.dot_general(a, b, dims, preferred_element_type=f32)


def ln_parts(v):
    centered = v - jnp.mean(v, axis=-1, keepdims=True)
    variance = jnp.mean(centered * centered, axis=-1, keepdims=True)
    return centered, lax.rsqrt(variance + NORM_EPS)


def ln_back(grad, xhat, rstd, gain):
    t = grad * gain
    m1 = jnp.mean(t, axis=-1, keepdims=True)
    m2 = jnp.mean(t * xhat, axis=-1, keepdims=True)
    return rstd * (t - m1 - xhat * m2)


def gelu_parts(u):
    cdf = 0.5 + 0.5 * lax.erf(u * (2.0**-0.5))
    density = jnp.exp2(u * u * (-0.5 * math.log2(math.e))) * (1.0 / math.sqrt(2 * math.pi))
    return u * cdf, cdf + u * density


def lane_left():
    return lax.broadcasted_iota(jnp.int32, (64, 128), 1) < 64


def two_heads(m, left):
    zero = jnp.zeros_like(m)
    return jnp.concatenate([jnp.where(left, m, zero), jnp.where(left, zero, m)], axis=0)


def diagonal(r, left):
    return jnp.where(left, r[0:64], r[64:128])


def attention_forward(i, mask, qkv, probs, mixed):
    left = lane_left()
    key = lax.broadcasted_iota(jnp.int32, (64, 64), 0)
    query = lax.broadcasted_iota(jnp.int32, (64, 64), 1)
    clouds = TB // 64
    rows = [pl.ds(pl.multiple_of(i * TB + 64 * c, 64), 64) for c in range(clouds)]
    units = [(c, g) for c in range(clouds) for g in range(3)]
    bias = []
    for c in range(clouds):
        allowed = (key <= query) & ((mask[i * clouds + c].T == 1) | (key == query))
        b = jnp.where(allowed, 0.0, -1e30)
        bias.append(jnp.concatenate([b, b], axis=1))
    held = {}
    for c, g in units:
        q = qkv[rows[c], D * g : D * g + 128] * jnp.asarray(0.125, bf16)
        k = qkv[rows[c], D * g + 128 : D * g + 256]
        held[c, g] = dot(k, two_heads(q, left), NT) + bias[c]
    for c, g in units:
        s = held[c, g]
        e = jnp.exp(s - jnp.max(s, axis=0, keepdims=True))
        p = e * (1.0 / jnp.sum(e, axis=0, keepdims=True))
        probs[rows[c], 128 * g : 128 * g + 128] = p
        held[c, g] = p.astype(bf16)
    for c, g in units:
        v = qkv[rows[c], D * g + 256 : D * g + 384]
        mixed[rows[c], 128 * g : 128 * g + 128] = diagonal(dot(held[c, g], v, TN), left).astype(bf16)


def attention_backward(i, g, qkv, probs, dmix, dqkv):
    left = lane_left()
    across = slice(128 * g, 128 * g + 128)
    rows = [pl.ds(pl.multiple_of(i * TA + 64 * c, 64), 64) for c in range(TA // 64)]
    held = []
    for r in rows:
        v = qkv[r, D * g + 256 : D * g + 384]
        held.append(dot(v, two_heads(dmix[r, across], left), NT))
    for c, r in enumerate(rows):
        p, dp = probs[r, across], held[c]
        held[c] = (p * (dp - jnp.sum(p * dp, axis=0, keepdims=True))).astype(bf16)
    for ds, r in zip(held, rows):
        q = qkv[r, D * g : D * g + 128] * jnp.asarray(0.125, bf16)
        k = qkv[r, D * g + 128 : D * g + 256]
        dv = dot(probs[r, across].astype(bf16), two_heads(dmix[r, across], left))
        dk = dot(ds, two_heads(q, left))
        dq = diagonal(dot(ds, k, TN), left) * 0.125
        dqkv[r, D * g : D * g + 128] = dq.astype(bf16)
        dqkv[r, D * g + 128 : D * g + 256] = dk.astype(bf16)
        dqkv[r, D * g + 256 : D * g + 384] = dv.astype(bf16)


def pick_rows(devs, total, shift, step, k, block=None):
    rows = total // devs[2]
    shape = (16 * devs[1], total if block is None else D)
    out = lax.broadcasted_iota(jnp.int32, shape, 0)
    col = lax.broadcasted_iota(jnp.int32, shape, 1)
    if block is not None:
        col = col + D * block
    dev = out >> 4
    i = out - 16 * dev - shift
    ok = (i >= 0) & (i < rows // step) & (col == rows * (dev + devs[0]) + step * i + k)
    return jnp.where(ok, 1.0, 0.0).astype(bf16)


class Layout:
    def __init__(self, n):
        self.n, self.R, self.Rd = n, D // n, FF // n
        R = self.R
        self.fold = 4 * R <= 16
        groups = [slice(D * k, D * k + D) for k in range(4)]
        if self.fold:
            self.u = [(groups[k], k * R, groups[0]) for k in range(4)]
            self.u_sums = [(groups[0], [(groups[k], k * R) for k in range(4)])]
        else:
            self.u = [(slice(0, FF), 0, slice(0, FF))]
            self.u_sums = [(slice(0, FF), [(slice(0, FF), 0)])]
        self.straight = self.Rd % 16 == 0
        self.blocks = ((16, D),) * 3 + ((16, D if self.fold else FF), (self.Rd if self.straight else 16, D))


def layer_kernel(dims, *refs):
    Z, Y, X = dims
    n = Z * Y * X * 2
    lay = Layout(n)
    R, Rd = lay.R, lay.Rd
    it = iter(refs)

    def take(count=None):
        return next(it) if count is None else [next(it) for _ in range(count)]

    x_hbm, dy_hbm, mask_hbm, wq_own, wp_own, wu_own, wd_own, vec_own = take(8)
    out_hbm, ig_hbm, gq_out, gu_out, gd_out, small_out, norm_out = take(7)
    x, dy, mask, a, qkv, probs, mixed, h1, dh1, c_all, z_all, du_all = take(12)
    bufs = take(6)
    wq, wp, wu, wd, vec, bu, vgrid, sel, tmp_d, tmp_q = take(10)
    stage = take(6)
    acc_p, dvec, dbu = take(3)
    r1, r2, r3 = take(5), take(5), take(5)
    small, s1, s2, s3, sq, sq_in = take(6)
    local_sem, ag_send, ag_recv, rs_send, rs_recv, ar_send, ar_recv, sq_send, sq_recv = take(9)
    outs = [gq_out.at[0], gq_out.at[1], gq_out.at[2], gu_out, gd_out]

    T = x.shape[0]
    V = vec_own.shape[1]
    steps = T // TB
    dp = lax.axis_index("dp")
    fs = lax.axis_index("fsdp")
    z, y = dp // Y, lax.rem(dp, Y)
    xx, core = fs // 2, lax.rem(fs, 2)

    loads = [
        pltpu.make_async_copy(x_hbm, x, local_sem.at[0]),
        pltpu.make_async_copy(mask_hbm, mask, local_sem.at[1]),
        pltpu.make_async_copy(dy_hbm, dy, local_sem.at[2]),
    ]
    for c in loads:
        c.start()

    chips = [
        (lax.rem(z + k // (X * Y), Z), lax.rem(y + k // X % Y, Y), lax.rem(xx + k % X, X)) for k in range(1, Z * Y * X)
    ]
    chip_ids = [(c[0] * Y + c[1], c[2] * 2 + core) for c in chips]
    in_z = [k * X * Y - 1 for k in range(1, Z)]
    in_p = list(range(X * Y - 1))
    z_peers, z_ids = [chips[k] for k in in_z], [chip_ids[k] for k in in_z]
    p_peers, p_ids = [chips[k] for k in in_p], [chip_ids[k] for k in in_p]
    c_id = (dp, fs + 1 - 2 * core)
    P1, P2 = len(z_ids), len(p_ids)

    barrier = pltpu.get_barrier_semaphore()
    for dev in chip_ids + [c_id]:
        pl.semaphore_signal(barrier, inc=1, device_id=dev, device_id_type=MESH)

    for s in stage:
        s[...] = jnp.zeros_like(s)
    for g in range(3):
        for j in range(3):
            stage[g][0:R, 128 * j : 128 * j + 128] = wq_own[:, D * j + 128 * g : D * j + 128 * g + 128]
    for i in range(R):
        stage[i % 3][R + i // 3 : R + i // 3 + 1] = wp_own[i : i + 1]
    for cols, shift, at in lay.u:
        stage[3][shift : shift + R, at] = wu_own[:, cols]
    stage[5][0:1, 0:V] = vec_own[...]
    stage[4][0:Rd] = wd_own[...]
    for g, s in zip(bufs, stage):
        g[z, y, xx, core] = s[...].astype(bf16)

    pl.semaphore_wait(barrier, len(chip_ids) + 1)

    def remote(src, dst, send, recv, dev):
        return pltpu.make_async_remote_copy(
            src_ref=src, dst_ref=dst, send_sem=send, recv_sem=recv, device_id=dev, device_id_type=MESH
        )

    def gather(ch, stage):
        g = bufs[ch]
        send, recv = ag_send.at[ch], ag_recv.at[ch]
        if stage == 0:
            own = g.at[z, y, xx, core]
            return [remote(own, own, send.at[j], recv.at[j], z_ids[j]) for j in range(P1)]
        if stage == 1:
            own = g.at[:, y, xx, core]
            return [remote(own, own, send.at[P1 + j], recv.at[P1 + j], p_ids[j]) for j in range(P2)]
        own = g.at[:, :, :, core]
        return [remote(own, own, send.at[P1 + P2], recv.at[P1 + P2], c_id)]

    def gather_step(ch, stage):
        if stage > 0:
            for c in gather(ch, stage - 1):
                c.wait()
        if stage < 3:
            for c in gather(ch, stage):
                c.start()

    def scatter(ch, stage):
        g = bufs[ch]
        send, recv = rs_send.at[ch], rs_recv.at[ch]
        if stage == 0:
            return [remote(g.at[:, :, :, 1 - core], r1[ch], send.at[P1 + P2], recv.at[P1 + P2], c_id)]
        if stage == 1:
            return [
                remote(g.at[:, p_peers[j][1], p_peers[j][2], core], r2[ch].at[j], send.at[P1 + j], recv.at[P1 + j], p_ids[j])
                for j in range(P2)
            ]
        return [
            remote(g.at[z_peers[j][0], y, xx, core], r3[ch].at[j], send.at[j], recv.at[j], z_ids[j]) for j in range(P1)
        ]

    def scatter_step(ch, stage):
        g = bufs[ch]
        if stage > 0:
            for c in scatter(ch, stage - 1):
                c.wait()
        if stage == 1:
            for zz in range(Z):
                for yy in range(Y):
                    for cx in range(X):
                        t = g[zz, yy, cx, core].astype(f32) + r1[ch][zz, yy, cx].astype(f32)
                        g[zz, yy, cx, core] = t.astype(bf16)
        elif stage == 2:
            for zz in range(Z):
                t = g[zz, y, xx, core].astype(f32)
                for j in range(P2):
                    t = t + r2[ch][j, zz].astype(f32)
                g[zz, y, xx, core] = t.astype(bf16)
        elif stage == 3:
            t = g[z, y, xx, core].astype(f32)
            for j in range(P1):
                t = t + r3[ch][j].astype(f32)
            outs[ch][...] = t
        if stage < 3:
            for c in scatter(ch, stage):
                c.start()

    per_z = 2 * X * Y
    z_group = max(1, min(Z, 32 // per_z))
    count = z_group * per_z
    n_groups = Z // z_group
    SEL = {(0, 1, 0): 0, (R, 3, 0): 1, (R, 3, 1): 2, (R, 3, 2): 3}

    def pick(k, rows, shift, step, first, block=None):
        if n_groups == 1 and (shift, step, first) in SEL and rows == D:
            return sel[SEL[shift, step, first]]
        return pick_rows((k * count, count, n), rows, shift, step, first, block)

    def by_groups(f):
        if n_groups == 1:
            f(0)
        else:
            pl.loop(0, n_groups)(f)

    def unpack(into, cols, terms):
        def part(k):
            total = None
            for g, at, rows, shift, step, first, block in terms:
                flat = g[pl.ds(k * z_group, z_group), :, :, :, :, at].reshape(16 * count, at.stop - at.start)
                t = dot(pick(k, rows, shift, step, first, block), flat, TN)
                total = t if total is None else total + t
            if n_groups == 1:
                into[:, cols] = total.astype(bf16)
            else:
                into[:, cols] = (into[:, cols].astype(f32) + total).astype(bf16)

        if n_groups > 1:
            into[:, cols] = jnp.zeros((into.shape[0], cols.stop - cols.start), bf16)
        by_groups(part)

    def pack(g, at, terms):
        def one(k):
            total = None
            for source, cols, rows, shift, step, first in terms:
                t = dot(pick(k, rows, shift, step, first), source[:, cols])
                total = t if total is None else total + t
            shape = (z_group,) + g.shape[1:5] + (total.shape[1],)
            g[pl.ds(k * z_group, z_group), :, :, :, :, at] = total.astype(bf16).reshape(shape)

        by_groups(one)

    every = slice(0, D)

    for ch in (5, 0, 1, 2):
        gather_step(ch, 0)
    if n_groups == 1:
        for (shift, step, first), k in SEL.items():
            sel[k] = pick_rows((0, n, n), D, shift, step, first)
    for r in (acc_p, dvec, dbu):
        r[...] = jnp.zeros_like(r)
    for c in loads:
        c.wait()
    for ch in (5, 0, 1, 2):
        gather_step(ch, 1)
    gather_step(3, 0)
    dvec[5:6] = jnp.sum(dy[...].astype(f32), axis=0, keepdims=True)
    for ch in (5, 0, 1, 2):
        gather_step(ch, 2)
    gather_step(3, 1)
    gather_step(4, 0)
    for ch in range(3):
        gather_step(ch, 3)
        unpack(wq, slice(D * ch, D * ch + D), [(bufs[ch], every, D, 0, 1, 0, None)])
    unpack(wp, every, [(bufs[k], every, D, R, 3, k, None) for k in range(3)])

    gather_step(5, 3)
    for k in range(n_groups):
        row = lax.broadcasted_iota(jnp.int32, (count, 16 * count), 0)
        col = lax.broadcasted_iota(jnp.int32, (count, 16 * count), 1)
        pick_vec = jnp.where(col == 16 * row, 1.0, 0.0).astype(bf16)
        flat = bufs[5][k * z_group : (k + 1) * z_group].reshape(16 * count, 128)
        vgrid[k * count : (k + 1) * count] = dot(pick_vec, flat)
    for d in range(n):
        start, stop = V * d, V * d + V
        while start < stop:
            r0, l0 = start // D, start % D
            size = min(stop - start, D - l0)
            o = start - V * d
            vec[r0 : r0 + 1, l0 : l0 + size] = vgrid[d : d + 1, o : o + size]
            start += size
    for k in range(FF // D):
        bu[:, D * k : D * k + D] = vec[6 + k : 7 + k]

    @pl.loop(0, steps)
    def _(i):
        @pl.when(i == 1)
        def _():
            gather_step(3, 2)
            gather_step(4, 1)

        rows = pl.ds(pl.multiple_of(i * TB, TB), TB)
        xv = x[rows, :].astype(f32)
        centered, rstd = ln_parts(xv)
        av = (centered * rstd * vec[0:1] + vec[1:2]).astype(bf16)
        a[rows, :] = av
        qkv[rows, :] = dot(av, wq[...]).astype(bf16)
        attention_forward(i, mask, qkv, probs, mixed)
        h1[rows, :] = xv + (dot(mixed[rows, :], wp[...]) + vec[4:5])

    gather_step(4, 2)
    gather_step(3, 3)
    for cols, shift, at in lay.u:
        unpack(wu, cols, [(bufs[3], at, D, shift, 1, 0, None)])
    gather_step(4, 3)
    if lay.straight:
        wd[...] = bufs[4][...].reshape(FF, D)
    else:
        for k in range(FF // D):
            unpack(wd.at[D * k : D * k + D], every, [(bufs[4], every, FF, 0, 1, 0, k)])

    @pl.loop(0, steps)
    def _(i):
        rows = pl.ds(pl.multiple_of(i * TB, TB), TB)
        centered, rstd = ln_parts(h1[rows, :])
        c = (centered * rstd * vec[2:3] + vec[3:4]).astype(bf16)
        c_all[rows, :] = c
        dyv = dy[rows, :]
        cuts = [slice(k * CH, (k + 1) * CH) for k in range(FF // CH)]
        ahead = dot(c, wu[:, cuts[0]]), dot(dyv, wd[cuts[0], :], NT)
        for k, ns in enumerate(cuts):
            u, dz = ahead
            if k + 1 < len(cuts):
                ahead = dot(c, wu[:, cuts[k + 1]]), dot(dyv, wd[cuts[k + 1], :], NT)
            zv, slope = gelu_parts(u + bu[:, ns])
            z_all[rows, ns] = zv.astype(bf16)
            du = (dz * slope).astype(bf16)
            du_all[rows, ns] = du
            dbu[:, ns] += jnp.sum(du.astype(f32), axis=0, keepdims=True)

    if lay.straight:
        bufs[4][...] = dot(dy[...], z_all[...], TN).astype(bf16).T.reshape(bufs[4].shape)
    else:
        tmp_d[...] = dot(dy[...], z_all[...], TN).astype(bf16).T
        pack(bufs[4], every, [(tmp_d, every, FF, 0, 1, 0)])
    scatter_step(4, 0)

    dmix = mixed

    @pl.loop(0, steps)
    def _(i):
        rows = pl.ds(pl.multiple_of(i * TB, TB), TB)
        dc = dot(du_all[rows, :], wu[...], NT)
        centered, rstd = ln_parts(h1[rows, :])
        xhat = centered * rstd
        dvec[2:3] += jnp.sum(dc * xhat, axis=0, keepdims=True)
        dvec[3:4] += jnp.sum(dc, axis=0, keepdims=True)
        d1 = dy[rows, :].astype(f32) + ln_back(dc, xhat, rstd, vec[2:3])
        dh1[rows, :] = d1
        dr = d1.astype(bf16)
        dvec[4:5] += jnp.sum(dr.astype(f32), axis=0, keepdims=True)
        acc_p[...] += dot(mixed[rows, :], dr, TN)
        dmix[rows, :] = dot(dr, wp[...], NT).astype(bf16)

    scatter_step(4, 1)
    wu[...] = dot(c_all[...], du_all[...], TN).astype(bf16)
    for at, terms in lay.u_sums:
        pack(bufs[3], at, [(wu, cols, D, shift, 1, 0) for cols, shift in terms])
    scatter_step(3, 0)
    wp[...] = acc_p[...].astype(bf16)

    dqkv = du_all

    for g in range(3):
        @pl.loop(0, T // TA)
        def _(i):
            attention_backward(i, g, qkv, probs, dmix, dqkv)

        if g == 0:
            scatter_step(3, 1)
        if g == 1:
            scatter_step(0, 1)
            scatter_step(4, 2)
        if g == 2:
            scatter_step(1, 1)
        tmp_q[...] = dot(a[...], dqkv[:, D * g : D * g + D], TN).astype(bf16)
        pack(bufs[g], every, [(tmp_q, every, D, 0, 1, 0), (wp, every, D, R, 3, g)])
        scatter_step(g, 0)

    @pl.loop(0, steps)
    def _(i):
        rows = pl.ds(pl.multiple_of(i * TB, TB), TB)
        da = dot(dqkv[rows, 0 : 3 * D], wq[...], NT)
        centered, rstd = ln_parts(x[rows, :].astype(f32))
        xhat = centered * rstd
        dvec[0:1] += jnp.sum(da * xhat, axis=0, keepdims=True)
        dvec[1:2] += jnp.sum(da, axis=0, keepdims=True)
        dh1[rows, :] = dh1[rows, :] + ln_back(da, xhat, rstd, vec[0:1])

    put_ig = pltpu.make_async_copy(dh1, ig_hbm, local_sem.at[4])
    put_ig.start()
    scatter_step(2, 1)
    scatter_step(3, 2)

    small[0] = jnp.zeros((16, D), f32)
    small[0, 0:6] = dvec[0:6]
    for k in range(FF // D):
        small[0, 6 + k : 7 + k] = dbu[:, D * k : D * k + D]
    received = (s1, s2, s3)

    def spread(stage):
        if stage == 0:
            return [remote(small.at[0], s1.at[j], ar_send.at[j], ar_recv.at[j], z_ids[j]) for j in range(P1)]
        if stage == 1:
            return [remote(small.at[1], s2.at[j], ar_send.at[P1 + j], ar_recv.at[P1 + j], p_ids[j]) for j in range(P2)]
        return [remote(small.at[2], s3.at[0], ar_send.at[P1 + P2], ar_recv.at[P1 + P2], c_id)]

    def spread_step(stage):
        if stage > 0:
            copies = spread(stage - 1)
            for c in copies:
                c.wait()
            t = small[stage - 1]
            for j in range(len(copies)):
                t = t + received[stage - 1][j]
            if stage < 3:
                small[stage] = t
            else:
                small_out[...] = t
        if stage < 3:
            for c in spread(stage):
                c.start()

    spread_step(0)

    @pl.loop(0, steps)
    def _(i):
        rows = pl.ds(pl.multiple_of(i * TB, TB), TB)
        dy[rows, :] = (h1[rows, :] + (dot(z_all[rows, :], wd[...]) + vec[5:6])).astype(bf16)

    put_out = pltpu.make_async_copy(dy, out_hbm, local_sem.at[3])
    put_out.start()

    scatter_step(0, 2)
    spread_step(1)
    scatter_step(1, 2)
    scatter_step(4, 3)
    scatter_step(2, 2)
    spread_step(2)
    scatter_step(3, 3)
    spread_step(3)
    for ch in range(3):
        scatter_step(ch, 3)

    squares = jnp.zeros((1, 1), f32)
    for ref in outs:
        t = ref[...]
        squares = squares + jnp.sum(jnp.sum(t * t, axis=0, keepdims=True), axis=1, keepdims=True)
    sq[0] = jnp.broadcast_to(squares, (8, 128))
    to_core = remote(sq.at[0], sq_in.at[len(chips)], sq_send.at[len(chips)], sq_recv.at[len(chips)], c_id)
    to_core.start()
    to_core.wait()
    sq[1] = sq[0] + sq_in[len(chips)]
    to_chips = [remote(sq.at[1], sq_in.at[j], sq_send.at[j], sq_recv.at[j], chip_ids[j]) for j in range(len(chips))]
    for c in to_chips:
        c.start()
    for c in to_chips:
        c.wait()
    total = sq[1]
    for j in range(len(chips)):
        total = total + sq_in[j]
    norm_out[...] = total
    put_out.wait()
    put_ig.wait()


def layer_call(dims, x, dy, masks, wq, wp, wu, wd, vec):
    Z, Y, X = dims
    n = Z * Y * X * 2
    lay = Layout(n)
    T = x.shape[0]
    S = jax.ShapeDtypeStruct
    V = pltpu.VMEM
    dma = pltpu.SemaphoreType.DMA
    vm = pl.BlockSpec(memory_space=pltpu.VMEM)
    hbm = pl.BlockSpec(memory_space=pl.ANY)
    P1, P2, chips = Z - 1, X * Y - 1, Z * Y * X - 1
    peers = P1 + P2 + 1
    blocks = lay.blocks
    one_group = Z * Y * X * 2 <= 32
    scratch = [V((T, D), bf16), V((T, D), bf16), V(masks.shape, jnp.int32), V((T, D), bf16), V((T, 3 * D), bf16)]
    scratch += [V((T, D), f32), V((T, D), bf16), V((T, D), f32), V((T, D), f32), V((T, D), bf16)]
    scratch += [V((T, FF), bf16), V((T, FF), bf16)]
    scratch += [V((Z, Y, X, 2) + b, bf16) for b in blocks + ((16, 128),)]
    scratch += [V((D, 3 * D), bf16), V((D, D), bf16), V((D, FF), bf16), V((FF, D), bf16), V((16, D), f32), V((1, FF), f32)]
    scratch += [V((n, 128), f32), V((4, 16 * n, D) if one_group else (1, 16, 128), bf16)]
    scratch += [V((16, 128) if lay.straight else (FF, D), bf16), V((D, D), bf16)]
    scratch += [V(b, f32) for b in blocks + ((16, 128),)]
    scratch += [V((D, D), f32), V((8, D), f32), V((1, FF), f32)]
    scratch += [V((Z, Y, X) + b, bf16) for b in blocks]
    scratch += [V((P2, Z) + b, bf16) for b in blocks]
    scratch += [V((P1,) + b, bf16) for b in blocks]
    scratch += [V((3, 16, D), f32), V((P1, 16, D), f32), V((P2, 16, D), f32), V((1, 16, D), f32)]
    scratch += [V((2, 8, 128), f32), V((chips + 1, 8, 128), f32)]
    scratch += [dma((5,))] + [dma((6, peers))] * 4 + [dma((peers,))] * 2 + [dma((chips + 1,))] * 2
    return pl.pallas_call(
        functools.partial(layer_kernel, dims),
        out_shape=[
            S((T, D), bf16), S((T, D), f32), S((3,) + blocks[0], f32), S(blocks[3], f32), S(blocks[4], f32),
            S((16, D), f32), S((8, 128), f32),
        ],
        in_specs=[hbm] * 3 + [vm] * 5,
        out_specs=[hbm] * 2 + [vm] * 5,
        scratch_shapes=scratch,
        compiler_params=pltpu.CompilerParams(
            collective_id=0, has_side_effects=True, vmem_limit_bytes=62 * 1024 * 1024
        ),
        name="layer",
    )(x, dy, masks, wq, wp, wu, wd, vec)


def adam_step(w, m, r, g, rate, decay):
    m_new = BETA1 * m + (1.0 - BETA1) * g
    r_new = BETA2 * r + (1.0 - BETA2) * g * g
    m_hat = m_new / (1.0 - BETA1**STEP)
    r_hat = r_new / (1.0 - BETA2**STEP)
    return w - rate * (m_hat / (jnp.sqrt(r_hat) + ADAM_EPS) + decay * w), m_new, r_new


def adam_kernel(n, *refs):
    small, matrix_squares, gq, gu, gd = refs[0:5]
    state = refs[5:20]
    out_in, ig_in = refs[20:22]
    out_ref, ig_ref, norm = refs[22:25]
    new = refs[25:40]
    sem, out_v, ig_v = refs[40:43]
    lay = Layout(n)
    R, Rd, V = lay.R, lay.Rd, state[12].shape[1]
    T = out_v.shape[0]
    parts = [pl.ds(k * (T // 4), T // 4) for k in range(4)]
    loads = [pltpu.make_async_copy(out_in.at[r], out_v.at[r], sem.at[k]) for k, r in enumerate(parts)]
    loads += [pltpu.make_async_copy(ig_in.at[r], ig_v.at[r], sem.at[4 + k]) for k, r in enumerate(parts)]
    stores = [pltpu.make_async_copy(out_v.at[r], out_ref.at[r], sem.at[8 + k]) for k, r in enumerate(parts)]
    stores += [pltpu.make_async_copy(ig_v.at[r], ig_ref.at[r], sem.at[12 + k]) for k, r in enumerate(parts)]
    for c in loads:
        c.start()
    for c, d in zip(loads, stores):
        c.wait()
        d.start()
    vecs = small[0:10]
    squares = jnp.sum(jnp.sum(vecs * vecs, axis=0, keepdims=True), axis=1, keepdims=True) + matrix_squares[0:1, 0:1]
    clip = jnp.sqrt(squares)
    norm[...] = clip
    factor = 1.0 / clip

    def step(k, rows, cols, g, rate, decay):
        w, m, r = (ref[rows, cols] for ref in state[3 * k : 3 * k + 3])
        for ref, value in zip(new[3 * k : 3 * k + 3], adam_step(w, m, r, g * factor, rate, decay)):
            ref[rows, cols] = value

    every = slice(0, D)
    g = jnp.concatenate([gq[k, 0:R, 128 * j : 128 * j + 128] for j in range(3) for k in range(3)], axis=1)
    step(0, slice(0, R), slice(0, 3 * D), g, RATES[0], DECAY)
    for i in range(R):
        step(1, slice(i, i + 1), every, gq[i % 3, R + i // 3 : R + i // 3 + 1], RATES[1], DECAY)
    for cols, shift, at in lay.u:
        step(2, slice(0, R), cols, gu[shift : shift + R, at], RATES[2], DECAY)
    step(3, slice(0, Rd), every, gd[0:Rd], RATES[3], DECAY)
    me = lax.axis_index("dp") * (n // lax.axis_size("dp")) + lax.axis_index("fsdp")
    start = me * V
    row, lane = start // D, lax.rem(start, D)
    two = jnp.concatenate([small[pl.ds(row, 1), :], small[pl.ds(row + 1, 1), :]], axis=1)
    two = pltpu.roll(jnp.broadcast_to(two, (8, 2 * D)), 2 * D - lane, 1)
    step(4, slice(0, 1), slice(0, V), two[0:1, 0:V], VECTOR_RATE, 0.0)
    for c in stores:
        c.wait()


def adam_call(n, small, squares, gq, gu, gd, state, out, ig):
    vm = pl.BlockSpec(memory_space=pltpu.VMEM)
    hbm = pl.BlockSpec(memory_space=pl.ANY)
    S = jax.ShapeDtypeStruct
    return pl.pallas_call(
        functools.partial(adam_kernel, n),
        out_shape=[S(out.shape, out.dtype), S(ig.shape, ig.dtype), S((1, 1), f32)] + [S(s.shape, f32) for s in state],
        in_specs=[vm] * 20 + [hbm] * 2,
        out_specs=[hbm] * 2 + [vm] * 16,
        scratch_shapes=[pltpu.SemaphoreType.DMA((16,)), pltpu.VMEM(out.shape, out.dtype), pltpu.VMEM(ig.shape, ig.dtype)],
        name="adam",
    )(small, squares, gq, gu, gd, *state, out, ig)


def solution(mesh):
    n_dp, n_fs = mesh.shape["dp"], mesh.shape["fsdp"]
    X = n_fs // 2
    Y = X if n_dp % X == 0 else 1
    dims = (n_dp // Y, Y, X)
    n = n_dp * n_fs

    def per_device(x, dy, masks, *state):
        state = list(state)
        flat = [s.shape for s in state[12:15]]
        state[12:15] = [s.reshape(1, -1) for s in state[12:15]]
        out, ig, gq, gu, gd, small, squares = layer_call(
            dims, x, dy, masks, state[0], state[3], state[6], state[9], state[12]
        )
        res = adam_call(n, small, squares, gq, gu, gd, state, out, ig)
        new = list(res[3:])
        new[12:15] = [v.reshape(f) for v, f in zip(new[12:15], flat)]
        return (res[0], res[1], res[2].reshape(()), *new)

    rows = P(("dp", "fsdp"), None)
    line = P(("dp", "fsdp"))
    placed = (rows, rows, P(("dp", "fsdp"), None, None)) + (rows,) * 12 + (line,) * 3
    given = (rows, rows, P()) + (rows,) * 12 + (line,) * 3
    return jax.shard_map(per_device, mesh=mesh, in_specs=placed, out_specs=given, check_vma=False)
```

```python
import functools
import math

import jax
import jax.numpy as jnp
from jax import lax
from jax.experimental import pallas as pl
from jax.experimental.pallas import tpu as pltpu
from jax.sharding import PartitionSpec as P

D = 384
FF = 1536
HD = 64
STEP = 10
NORM_EPS = 1e-05
BETA1 = 0.9
BETA2 = 0.999
ADAM_EPS = 1e-08
DECAY = 0.05
RATES = (0.1, 0.5, 0.1, 0.05)
VECTOR_RATE = 1.0
TB = 512
TA = 1024
TM = 1024
CH = 256

f32 = jnp.float32
bf16 = jnp.bfloat16
NN = (((1,), (0,)), ((), ()))
NT = (((1,), (1,)), ((), ()))
TN = (((0,), (0,)), ((), ()))
MESH = pl.DeviceIdType.MESH


def dot(a, b, dims=NN):
    return lax.dot_general(a, b, dims, preferred_element_type=f32)


def ln_parts(v):
    centered = v - jnp.mean(v, axis=-1, keepdims=True)
    variance = jnp.mean(centered * centered, axis=-1, keepdims=True)
    return centered, lax.rsqrt(variance + NORM_EPS)


def ln_back(grad, xhat, rstd, gain):
    t = grad * gain
    m1 = jnp.mean(t, axis=-1, keepdims=True)
    m2 = jnp.mean(t * xhat, axis=-1, keepdims=True)
    return rstd * (t - m1 - xhat * m2)


def gelu_parts(u):
    cdf = 0.5 + 0.5 * lax.erf(u * (2.0**-0.5))
    density = jnp.exp2(u * u * (-0.5 * math.log2(math.e))) * (1.0 / math.sqrt(2 * math.pi))
    return u * cdf, cdf + u * density


def lane_left():
    return lax.broadcasted_iota(jnp.int32, (64, 128), 1) < 64


def two_heads(m, left):
    zero = jnp.zeros_like(m)
    return jnp.concatenate([jnp.where(left, m, zero), jnp.where(left, zero, m)], axis=0)


def diagonal(r, left):
    return jnp.where(left, r[0:64], r[64:128])


def attention_forward(i, g, mask, qkv, probs, mixed):
    left = lane_left()
    across = slice(128 * g, 128 * g + 128)
    clouds = TA // 64
    rows = [pl.ds(pl.multiple_of(i * TA + 64 * c, 64), 64) for c in range(clouds)]
    held = []
    for c, r in enumerate(rows):
        b = jnp.where(mask[i * clouds + c] == 1, 0.0, -1e30)
        q = qkv[r, D * g : D * g + 128] * jnp.asarray(0.125, bf16)
        k = qkv[r, D * g + 128 : D * g + 256]
        held.append(dot(k, two_heads(q, left), NT) + jnp.concatenate([b, b], axis=1))
    for c, r in enumerate(rows):
        s = held[c]
        e = jnp.exp(s - jnp.max(s, axis=0, keepdims=True))
        p = e * (1.0 / jnp.sum(e, axis=0, keepdims=True))
        probs[r, across] = p
        held[c] = p.astype(bf16)
    for c, r in enumerate(rows):
        v = qkv[r, D * g + 256 : D * g + 384]
        mixed[r, across] = diagonal(dot(held[c], v, TN), left).astype(bf16)


def attention_backward(i, g, qkv, probs, dmix, dqkv):
    left = lane_left()
    across = slice(128 * g, 128 * g + 128)
    rows = [pl.ds(pl.multiple_of(i * TA + 64 * c, 64), 64) for c in range(TA // 64)]
    held = []
    for r in rows:
        v = qkv[r, D * g + 256 : D * g + 384]
        held.append(dot(v, two_heads(dmix[r, across], left), NT))
    for c, r in enumerate(rows):
        p, dp = probs[r, across], held[c]
        held[c] = (p * (dp - jnp.sum(p * dp, axis=0, keepdims=True))).astype(bf16)
    for ds, r in zip(held, rows):
        q = qkv[r, D * g : D * g + 128] * jnp.asarray(0.125, bf16)
        k = qkv[r, D * g + 128 : D * g + 256]
        dv = dot(probs[r, across].astype(bf16), two_heads(dmix[r, across], left))
        dk = dot(ds, two_heads(q, left))
        dq = diagonal(dot(ds, k, TN), left) * 0.125
        dqkv[r, D * g : D * g + 128] = dq.astype(bf16)
        dqkv[r, D * g + 128 : D * g + 256] = dk.astype(bf16)
        dqkv[r, D * g + 256 : D * g + 384] = dv.astype(bf16)


def pick_rows(devs, total, shift, step, k, block=None):
    rows = total // devs[2]
    shape = (16 * devs[1], total if block is None else D)
    out = lax.broadcasted_iota(jnp.int32, shape, 0)
    col = lax.broadcasted_iota(jnp.int32, shape, 1)
    if block is not None:
        col = col + D * block
    dev = out >> 4
    i = out - 16 * dev - shift
    ok = (i >= 0) & (i < rows // step) & (col == rows * (dev + devs[0]) + step * i + k)
    return jnp.where(ok, 1.0, 0.0).astype(bf16)


class Layout:
    def __init__(self, n):
        self.n, self.R, self.Rd = n, D // n, FF // n
        self.straight = self.Rd % 16 == 0
        self.cuts = self.Rd // 16 if self.straight else 1
        self.cw = FF // self.cuts
        self.up = self.cw if self.straight else D
        if self.straight:
            self.pieces = [
                (self.Rd * d + 16 * k, self.cw * k + 16 * d, k, 16 * d) for k in range(self.cuts) for d in range(n)
            ]
        self.blocks = ((16, D),) * 3 + ((16, self.up + D),) * self.cuts
        self.chunks = len(self.blocks)


def layer_kernel(dims, *refs):
    Z, Y, X = dims
    n = Z * Y * X * 2
    lay = Layout(n)
    R, Rd, NC, VEC = lay.R, lay.Rd, lay.chunks, lay.chunks
    MLP = list(range(3, NC))
    it = iter(refs)

    def take(count=None):
        return next(it) if count is None else [next(it) for _ in range(count)]

    x_hbm, dy_hbm, mask_hbm, wq_own, wp_own, wu_own, wd_own, vec_own = take(8)
    out_hbm, ig_hbm, gq_out, gm_out, small_out, norm_out = take(6)
    x, dy, mask, a, qkv, probs, mixed, h1, dh1, c_all, z_all, du_all = take(12)
    bufs = take(NC + 1)
    wq, wp, wu, wd, vec, bu, vgrid, sel, tmp_q = take(9)
    stage = take(NC + 1)
    acc_p, dvec, dbu = take(3)
    r1, r2, r3 = take(NC), take(NC), take(NC)
    small, s1, s2, s3, sq, sq_in = take(6)
    local_sem, ag_send, ag_recv, rs_send, rs_recv, ar_send, ar_recv, sq_send, sq_recv = take(9)
    outs = [gq_out.at[k] for k in range(3)] + [gm_out.at[k] for k in range(lay.cuts)]

    T = x.shape[0]
    V = vec_own.shape[1]
    dp = lax.axis_index("dp")
    fs = lax.axis_index("fsdp")
    z, y = dp // Y, lax.rem(dp, Y)
    xx, core = fs // 2, lax.rem(fs, 2)

    loads = [
        pltpu.make_async_copy(x_hbm, x, local_sem.at[0]),
        pltpu.make_async_copy(mask_hbm, mask, local_sem.at[1]),
        pltpu.make_async_copy(dy_hbm, dy, local_sem.at[2]),
    ]
    for c in loads:
        c.start()

    chips = [
        (lax.rem(z + k // (X * Y), Z), lax.rem(y + k // X % Y, Y), lax.rem(xx + k % X, X)) for k in range(1, Z * Y * X)
    ]
    chip_ids = [(c[0] * Y + c[1], c[2] * 2 + core) for c in chips]
    in_z = [k * X * Y - 1 for k in range(1, Z)]
    in_p = list(range(X * Y - 1))
    z_peers, z_ids = [chips[k] for k in in_z], [chip_ids[k] for k in in_z]
    p_peers, p_ids = [chips[k] for k in in_p], [chip_ids[k] for k in in_p]
    c_id = (dp, fs + 1 - 2 * core)
    P1, P2 = len(z_ids), len(p_ids)

    barrier = pltpu.get_barrier_semaphore()
    for dev in chip_ids + [c_id]:
        pl.semaphore_signal(barrier, inc=1, device_id=dev, device_id_type=MESH)

    for t in stage:
        t[...] = jnp.zeros_like(t)
    for g in range(3):
        for j in range(3):
            stage[g][0:R, 128 * j : 128 * j + 128] = wq_own[:, D * j + 128 * g : D * j + 128 * g + 128]
    for i in range(R):
        stage[i % 3][R + i // 3 : R + i // 3 + 1] = wp_own[i : i + 1]
    stage[VEC][0:1, 0:V] = vec_own[...]
    for ch in (0, 1, 2, VEC):
        bufs[ch][z, y, xx, core] = stage[ch][...].astype(bf16)

    pl.semaphore_wait(barrier, len(chip_ids) + 1)

    def remote(src, dst, send, recv, dev):
        return pltpu.make_async_remote_copy(
            src_ref=src, dst_ref=dst, send_sem=send, recv_sem=recv, device_id=dev, device_id_type=MESH
        )

    def gather(ch, stage):
        g = bufs[ch]
        send, recv = ag_send.at[ch], ag_recv.at[ch]
        if stage == 0:
            own = g.at[z, y, xx, core]
            return [remote(own, own, send.at[j], recv.at[j], z_ids[j]) for j in range(P1)]
        if stage == 1:
            own = g.at[:, y, xx, core]
            return [remote(own, own, send.at[P1 + j], recv.at[P1 + j], p_ids[j]) for j in range(P2)]
        own = g.at[:, :, :, core]
        return [remote(own, own, send.at[P1 + P2], recv.at[P1 + P2], c_id)]

    def gather_step(ch, stage):
        if stage > 0:
            for c in gather(ch, stage - 1):
                c.wait()
        if stage < 3:
            for c in gather(ch, stage):
                c.start()

    def scatter(ch, stage):
        g = bufs[ch]
        send, recv = rs_send.at[ch], rs_recv.at[ch]
        if stage == 0:
            return [remote(g.at[:, :, :, 1 - core], r1[ch], send.at[P1 + P2], recv.at[P1 + P2], c_id)]
        if stage == 1:
            return [
                remote(g.at[:, p_peers[j][1], p_peers[j][2], core], r2[ch].at[j], send.at[P1 + j], recv.at[P1 + j], p_ids[j])
                for j in range(P2)
            ]
        return [
            remote(g.at[z_peers[j][0], y, xx, core], r3[ch].at[j], send.at[j], recv.at[j], z_ids[j]) for j in range(P1)
        ]

    def scatter_step(ch, stage):
        g = bufs[ch]
        if stage > 0:
            for c in scatter(ch, stage - 1):
                c.wait()
        if stage == 1:
            @pl.loop(0, Z)
            def _(zz):
                for yy in range(Y):
                    for cx in range(X):
                        t = g[zz, yy, cx, core].astype(f32) + r1[ch][zz, yy, cx].astype(f32)
                        g[zz, yy, cx, core] = t.astype(bf16)
        elif stage == 2:
            for zz in range(Z):
                t = g[zz, y, xx, core].astype(f32)
                for j in range(P2):
                    t = t + r2[ch][j, zz].astype(f32)
                g[zz, y, xx, core] = t.astype(bf16)
        elif stage == 3:
            t = g[z, y, xx, core].astype(f32)
            for j in range(P1):
                t = t + r3[ch][j].astype(f32)
            outs[ch][...] = t
        if stage < 3:
            for c in scatter(ch, stage):
                c.start()

    per_z = 2 * X * Y
    z_group = max(1, min(Z, 32 // per_z))
    count = z_group * per_z
    n_groups = Z // z_group
    SEL = {(0, 1, 0): 0, (R, 3, 0): 1, (R, 3, 1): 2, (R, 3, 2): 3}

    def pick(k, rows, shift, step, first, block=None):
        if n_groups == 1 and (shift, step, first) in SEL and rows == D:
            return sel[SEL[shift, step, first]]
        return pick_rows((k * count, count, n), rows, shift, step, first, block)

    def by_groups(f):
        if n_groups == 1:
            f(0)
        else:
            pl.loop(0, n_groups)(f)

    def unpack(into, cols, terms):
        def part(k):
            total = None
            for g, at, rows, shift, step, first, block in terms:
                flat = g[pl.ds(k * z_group, z_group), :, :, :, :, at].reshape(16 * count, at.stop - at.start)
                t = dot(pick(k, rows, shift, step, first, block), flat, TN)
                total = t if total is None else total + t
            if n_groups == 1:
                into[:, cols] = total.astype(bf16)
            else:
                into[:, cols] = (into[:, cols].astype(f32) + total).astype(bf16)

        if n_groups > 1:
            into[:, cols] = jnp.zeros((into.shape[0], cols.stop - cols.start), bf16)
        by_groups(part)

    def pack(g, at, terms, more=False):
        def one(k):
            total = None
            for source, rows, shift, step, first, block in terms:
                t = dot(pick(k, rows, shift, step, first, block), source[...])
                total = t if total is None else total + t
            where = pl.ds(k * z_group, z_group)
            total = total.reshape((z_group,) + g.shape[1:5] + (total.shape[1],))
            if more:
                total = total + g[where, :, :, :, :, at].astype(f32)
            g[where, :, :, :, :, at] = total.astype(bf16)

        by_groups(one)

    every = slice(0, D)

    for ch in (VEC, 0, 1, 2):
        gather_step(ch, 0)
    if lay.straight:
        for nat, _, k, at in lay.pieces:
            stage[3 + k][0:R, at : at + 16] = wu_own[:, nat : nat + 16]
        for k in range(lay.cuts):
            stage[3 + k][:, lay.up : lay.up + D] = wd_own[16 * k : 16 * k + 16]
    else:
        for k in range(FF // D):
            stage[3][R * k : R * k + R, 0:D] = wu_own[:, D * k : D * k + D]
        stage[3][0:Rd, D : 2 * D] = wd_own[...]
    for ch in MLP:
        bufs[ch][z, y, xx, core] = stage[ch][...].astype(bf16)
        gather_step(ch, 0)
    if n_groups == 1:
        for (shift, step, first), k in SEL.items():
            sel[k] = pick_rows((0, n, n), D, shift, step, first)
    for r in (acc_p, dvec, dbu):
        r[...] = jnp.zeros_like(r)
    for c in loads:
        c.wait()

    @pl.loop(0, T // TB)
    def _(i):
        rows = pl.ds(pl.multiple_of(i * TB, TB), TB)
        centered, rstd = ln_parts(x[rows, :].astype(f32))
        h1[rows, :] = centered * rstd
        key = lax.broadcasted_iota(jnp.int32, (64, 64), 0)
        query = lax.broadcasted_iota(jnp.int32, (64, 64), 1)
        clouds = TB // 64
        for c in range(clouds):
            allowed = (key <= query) & ((mask[i * clouds + c].T == 1) | (key == query))
            mask[i * clouds + c] = jnp.where(allowed, 1, 0)

    for ch in (VEC, 0, 1, 2):
        gather_step(ch, 1)
    gather_step(MLP[0], 1)
    dvec[5:6] = jnp.sum(dy[...].astype(f32), axis=0, keepdims=True)
    gather_step(VEC, 2)
    gather_step(0, 2)
    gather_step(VEC, 3)
    for k in range(n_groups):
        row = lax.broadcasted_iota(jnp.int32, (count, 16 * count), 0)
        col = lax.broadcasted_iota(jnp.int32, (count, 16 * count), 1)
        pick_vec = jnp.where(col == 16 * row, 1.0, 0.0).astype(bf16)
        flat = bufs[VEC][k * z_group : (k + 1) * z_group].reshape(16 * count, 128)
        vgrid[k * count : (k + 1) * count] = dot(pick_vec, flat)
    for d in range(n):
        start, stop = V * d, V * d + V
        while start < stop:
            r0, l0 = start // D, start % D
            size = min(stop - start, D - l0)
            o = start - V * d
            vec[r0 : r0 + 1, l0 : l0 + size] = vgrid[d : d + 1, o : o + size]
            start += size

    def pair_forward(g):
        gather_step(g, 3)
        mine = slice(D * g, D * g + D)
        unpack(wq, mine, [(bufs[g], every, D, 0, 1, 0, None)])

        @pl.loop(0, T // TA)
        def _(i):
            @pl.when(i == 1)
            def _():
                if g < 2:
                    gather_step(g + 1, 2)
                    if len(MLP) > g + 1:
                        gather_step(MLP[g + 1], 1)
                else:
                    gather_step(MLP[0], 2)

            rows = pl.ds(pl.multiple_of(i * TA, TA), TA)
            if g == 0:
                av = (h1[rows, :] * vec[0:1] + vec[1:2]).astype(bf16)
                a[rows, :] = av
            else:
                av = a[rows, :]
            qkv[rows, mine] = dot(av, wq[:, mine]).astype(bf16)
            attention_forward(i, g, mask, qkv, probs, mixed)

    for g in range(3):
        pair_forward(g)
    unpack(wp, every, [(bufs[k], every, D, R, 3, k, None) for k in range(3)])
    if lay.straight:
        for nat, place, _, _ in lay.pieces:
            r0, l0 = 6 + nat // D, nat % D
            bu[:, place : place + 16] = vec[r0 : r0 + 1, l0 : l0 + 16]
    else:
        for k in range(FF // D):
            bu[:, D * k : D * k + D] = vec[6 + k : 7 + k]

    @pl.loop(0, T // TB)
    def _(i):
        @pl.when(i == 2)
        def _():
            if len(MLP) > 1:
                gather_step(MLP[1], 2)

        rows = pl.ds(pl.multiple_of(i * TB, TB), TB)
        h = x[rows, :].astype(f32) + (dot(mixed[rows, :], wp[...]) + vec[4:5])
        h1[rows, :] = h
        centered, rstd = ln_parts(h)
        c_all[rows, :] = (centered * rstd * vec[2:3] + vec[3:4]).astype(bf16)

    for k in range(lay.cuts):
        ch = 3 + k
        cut = slice(lay.cw * k, lay.cw * k + lay.cw)
        gather_step(ch, 3)
        if lay.straight:
            unpack(wu, cut, [(bufs[ch], slice(0, lay.up), D, 0, 1, 0, None)])
            wd[cut, :] = bufs[ch][:, :, :, :, :, lay.up : lay.up + D].reshape(lay.cw, D)
        else:
            for j in range(FF // D):
                unpack(wu, slice(D * j, D * j + D), [(bufs[ch], every, D, R * j, 1, 0, None)])
                unpack(wd.at[D * j : D * j + D], every, [(bufs[ch], slice(D, 2 * D), FF, 0, 1, 0, j)])

        @pl.loop(0, T // TM)
        def _(i):
            @pl.when(i == 1)
            def _():
                if k == 0 and lay.cuts > 2:
                    gather_step(MLP[2], 2)
                if k > 0:
                    scatter_step(ch - 1, 1)

            rows = pl.ds(pl.multiple_of(i * TM, TM), TM)
            c, dyv = c_all[rows, :], dy[rows, :]
            for start in range(cut.start, cut.stop, CH):
                ns = slice(start, start + CH)
                u = dot(c, wu[:, ns]) + bu[:, ns]
                dz = dot(dyv, wd[ns, :], NT)
                zv, slope = gelu_parts(u)
                z_all[rows, ns] = zv.astype(bf16)
                du = (dz * slope).astype(bf16)
                du_all[rows, ns] = du
                dbu[:, ns] += jnp.sum(du.astype(f32), axis=0, keepdims=True)

        if lay.straight:
            g = bufs[ch]
            down = dot(dy[...], z_all[:, cut], TN).astype(bf16).T
            g[:, :, :, :, :, lay.up : lay.up + D] = down.reshape(g.shape[:5] + (D,))
            pack(g, slice(0, lay.up), [(dot(c_all[...], du_all[:, cut], TN).astype(bf16), D, 0, 1, 0, None)])
        else:
            for j in range(FF // D):
                cols = slice(D * j, D * j + D)
                tmp_q[...] = dot(dy[...], z_all[:, cols], TN).astype(bf16).T
                pack(bufs[ch], slice(D, 2 * D), [(tmp_q, FF, 0, 1, 0, j)], j > 0)
                tmp_q[...] = dot(c_all[...], du_all[:, cols], TN).astype(bf16)
                pack(bufs[ch], every, [(tmp_q, D, R * j, 1, 0, None)], j > 0)
        scatter_step(ch, 0)

    dmix = mixed

    @pl.loop(0, T // TM)
    def _(i):
        @pl.when(i == 1)
        def _():
            scatter_step(MLP[-1], 1)
            if len(MLP) > 1:
                scatter_step(MLP[0], 2)

        rows = pl.ds(pl.multiple_of(i * TM, TM), TM)
        dc = dot(du_all[rows, :], wu[...], NT)
        centered, rstd = ln_parts(h1[rows, :])
        xhat = centered * rstd
        dvec[2:3] += jnp.sum(dc * xhat, axis=0, keepdims=True)
        dvec[3:4] += jnp.sum(dc, axis=0, keepdims=True)
        d1 = dy[rows, :].astype(f32) + ln_back(dc, xhat, rstd, vec[2:3])
        dh1[rows, :] = d1
        dr = d1.astype(bf16)
        dvec[4:5] += jnp.sum(dr.astype(f32), axis=0, keepdims=True)
        acc_p[...] += dot(mixed[rows, :], dr, TN)
        dmix[rows, :] = dot(dr, wp[...], NT).astype(bf16)

    wp[...] = acc_p[...].astype(bf16)

    small[0] = jnp.zeros((16, D), f32)
    small[0, 2:6] = dvec[2:6]
    if lay.straight:
        for nat, place, _, _ in lay.pieces:
            r0, l0 = 6 + nat // D, nat % D
            small[0, r0 : r0 + 1, l0 : l0 + 16] = dbu[:, place : place + 16]
    else:
        for k in range(FF // D):
            small[0, 6 + k : 7 + k] = dbu[:, D * k : D * k + D]
    received = (s1, s2, s3)

    def spread(stage):
        if stage == 0:
            return [remote(small.at[0], s1.at[j], ar_send.at[j], ar_recv.at[j], z_ids[j]) for j in range(P1)]
        if stage == 1:
            return [remote(small.at[1], s2.at[j], ar_send.at[P1 + j], ar_recv.at[P1 + j], p_ids[j]) for j in range(P2)]
        return [remote(small.at[2], s3.at[0], ar_send.at[P1 + P2], ar_recv.at[P1 + P2], c_id)]

    def spread_step(stage):
        if stage > 0:
            copies = spread(stage - 1)
            for c in copies:
                c.wait()
            t = small[stage - 1]
            for j in range(len(copies)):
                t = t + received[stage - 1][j]
            if stage < 3:
                small[stage] = t
            else:
                small_out[...] = t
        if stage < 3:
            for c in spread(stage):
                c.start()

    spread_step(0)

    dqkv = du_all

    def pair_backward(g):
        @pl.loop(0, T // TA)
        def _(i):
            attention_backward(i, g, qkv, probs, dmix, dqkv)

        if g == 0 and len(MLP) > 2:
            scatter_step(MLP[1], 2)
        if g == 2:
            spread_step(1)
        if g > 0:
            scatter_step(g - 1, 1)
        if g == 1 and len(MLP) > 1:
            scatter_step(MLP[0], 3)
        if g == 2:
            scatter_step(MLP[-1], 2)
        tmp_q[...] = dot(a[...], dqkv[:, D * g : D * g + D], TN).astype(bf16)
        pack(bufs[g], every, [(tmp_q, D, 0, 1, 0, None), (wp, D, R, 3, g, None)])
        scatter_step(g, 0)

    for g in range(3):
        pair_backward(g)

    @pl.loop(0, T // TB)
    def _(i):
        @pl.when(i == 1)
        def _():
            scatter_step(2, 1)
            scatter_step(0, 2)

        @pl.when(i == 3)
        def _():
            if len(MLP) > 2:
                scatter_step(MLP[1], 3)
            scatter_step(1, 2)
            spread_step(2)

        rows = pl.ds(pl.multiple_of(i * TB, TB), TB)
        da = dot(dqkv[rows, 0 : 3 * D], wq[...], NT)
        centered, rstd = ln_parts(x[rows, :].astype(f32))
        xhat = centered * rstd
        dvec[0:1] += jnp.sum(da * xhat, axis=0, keepdims=True)
        dvec[1:2] += jnp.sum(da, axis=0, keepdims=True)
        dh1[rows, :] = dh1[rows, :] + ln_back(da, xhat, rstd, vec[0:1])

    put_ig = pltpu.make_async_copy(dh1, ig_hbm, local_sem.at[4])
    put_ig.start()

    @pl.loop(0, T // TB)
    def _(i):
        @pl.when(i == 1)
        def _():
            scatter_step(MLP[-1], 3)
            scatter_step(0, 3)

        @pl.when(i == 2)
        def _():
            scatter_step(2, 2)

        rows = pl.ds(pl.multiple_of(i * TB, TB), TB)
        dy[rows, :] = (h1[rows, :] + (dot(z_all[rows, :], wd[...]) + vec[5:6])).astype(bf16)

    put_out = pltpu.make_async_copy(dy, out_hbm, local_sem.at[3])
    put_out.start()

    squares = jnp.zeros((1, 1), f32)
    spread_step(3)
    for ch in MLP + [0, 1, 2]:
        if ch in (1, 2):
            scatter_step(ch, 3)
        t = outs[ch][...]
        squares = squares + jnp.sum(jnp.sum(t * t, axis=0, keepdims=True), axis=1, keepdims=True)
    for j in range(6):
        sq[0, j : j + 1] = dvec[j // 3 : j // 3 + 1, 128 * (j % 3) : 128 * (j % 3) + 128]
    sq[0, 6:8] = jnp.broadcast_to(squares, (2, 128))
    to_core = remote(sq.at[0], sq_in.at[len(chips)], sq_send.at[len(chips)], sq_recv.at[len(chips)], c_id)
    to_core.start()
    to_core.wait()
    sq[1] = sq[0] + sq_in[len(chips)]
    to_chips = [remote(sq.at[1], sq_in.at[j], sq_send.at[j], sq_recv.at[j], chip_ids[j]) for j in range(len(chips))]
    for c in to_chips:
        c.start()
    for c in to_chips:
        c.wait()
    total = sq[1]
    for j in range(len(chips)):
        total = total + sq_in[j]
    norm_out[...] = total
    for j in range(6):
        small_out[j // 3 : j // 3 + 1, 128 * (j % 3) : 128 * (j % 3) + 128] = total[j : j + 1]
    put_out.wait()
    put_ig.wait()


def layer_call(dims, x, dy, masks, wq, wp, wu, wd, vec):
    Z, Y, X = dims
    n = Z * Y * X * 2
    lay = Layout(n)
    T = x.shape[0]
    S = jax.ShapeDtypeStruct
    V = pltpu.VMEM
    dma = pltpu.SemaphoreType.DMA
    vm = pl.BlockSpec(memory_space=pltpu.VMEM)
    hbm = pl.BlockSpec(memory_space=pl.ANY)
    P1, P2, chips = Z - 1, X * Y - 1, Z * Y * X - 1
    peers = P1 + P2 + 1
    blocks, NC = lay.blocks, lay.chunks
    one_group = n <= 32
    scratch = [V((T, D), bf16), V((T, D), bf16), V(masks.shape, jnp.int32), V((T, D), bf16), V((T, 3 * D), bf16)]
    scratch += [V((T, D), f32), V((T, D), bf16), V((T, D), f32), V((T, D), f32), V((T, D), bf16)]
    scratch += [V((T, FF), bf16), V((T, FF), bf16)]
    scratch += [V((Z, Y, X, 2) + b, bf16) for b in blocks + ((16, 128),)]
    scratch += [V((D, 3 * D), bf16), V((D, D), bf16), V((D, FF), bf16), V((FF, D), bf16), V((16, D), f32), V((1, FF), f32)]
    scratch += [V((n, 128), f32), V((4, 16 * n, D) if one_group else (1, 16, 128), bf16), V((D, D), bf16)]
    scratch += [V(b, f32) for b in blocks + ((16, 128),)]
    scratch += [V((D, D), f32), V((8, D), f32), V((1, FF), f32)]
    scratch += [V((Z, Y, X) + b, bf16) for b in blocks]
    scratch += [V((P2, Z) + b, bf16) for b in blocks]
    scratch += [V((P1,) + b, bf16) for b in blocks]
    scratch += [V((3, 16, D), f32), V((P1, 16, D), f32), V((P2, 16, D), f32), V((1, 16, D), f32)]
    scratch += [V((2, 8, 128), f32), V((chips + 1, 8, 128), f32)]
    scratch += [dma((5,))] + [dma((NC + 1, peers))] * 4 + [dma((peers,))] * 2 + [dma((chips + 1,))] * 2
    return pl.pallas_call(
        functools.partial(layer_kernel, dims),
        out_shape=[
            S((T, D), bf16), S((T, D), f32), S((3,) + blocks[0], f32), S((lay.cuts,) + blocks[3], f32),
            S((16, D), f32), S((8, 128), f32),
        ],
        in_specs=[hbm] * 3 + [vm] * 5,
        out_specs=[hbm] * 2 + [vm] * 4,
        scratch_shapes=scratch,
        compiler_params=pltpu.CompilerParams(
            collective_id=0, has_side_effects=True, vmem_limit_bytes=62 * 1024 * 1024
        ),
        name="layer",
    )(x, dy, masks, wq, wp, wu, wd, vec)


def adam_step(w, m, r, g, rate, decay):
    m_new = BETA1 * m + (1.0 - BETA1) * g
    r_new = BETA2 * r + (1.0 - BETA2) * g * g
    m_hat = m_new / (1.0 - BETA1**STEP)
    r_hat = r_new / (1.0 - BETA2**STEP)
    return w - rate * (m_hat / (jnp.sqrt(r_hat) + ADAM_EPS) + decay * w), m_new, r_new


def adam_kernel(n, *refs):
    small, matrix_squares, gq, gm = refs[0:4]
    state = refs[4:19]
    out_in, ig_in = refs[19:21]
    out_ref, ig_ref, norm = refs[21:24]
    new_hbm = refs[24:39]
    sem, out_v, ig_v, up = refs[39:43]
    new = refs[43:58]
    lay = Layout(n)
    R, Rd, V = lay.R, lay.Rd, state[12].shape[1]
    T = out_v.shape[0]
    pieces = 4
    parts = [pl.ds(k * (T // pieces), T // pieces) for k in range(pieces)]
    moves = [(a, b, c, r) for r in parts for a, b, c in ((ig_in, ig_v, ig_ref), (out_in, out_v, out_ref))]
    loads = [pltpu.make_async_copy(a.at[r], b.at[r], sem.at[k]) for k, (a, b, c, r) in enumerate(moves)]
    stores = [pltpu.make_async_copy(b.at[r], c.at[r], sem.at[k + len(moves)]) for k, (a, b, c, r) in enumerate(moves)]
    for c in loads:
        c.start()
    puts = [pltpu.make_async_copy(a, b, sem.at[2 * len(moves) + k]) for k, (a, b) in enumerate(zip(new, new_hbm))]
    vecs = small[0:10]
    squares = jnp.sum(jnp.sum(vecs * vecs, axis=0, keepdims=True), axis=1, keepdims=True) + matrix_squares[6:7, 0:1]
    clip = jnp.sqrt(squares)
    norm[...] = clip
    factor = 1.0 / clip

    def step(k, rows, cols, g, rate, decay):
        w, m, r = (ref[rows, cols] for ref in state[3 * k : 3 * k + 3])
        for ref, value in zip(new[3 * k : 3 * k + 3], adam_step(w, m, r, g * factor, rate, decay)):
            ref[rows, cols] = value

    def put(k):
        for c in puts[3 * k : 3 * k + 3]:
            c.start()

    for c, d in zip(loads, stores):
        c.wait()
        d.start()
    every = slice(0, D)
    if lay.straight:
        for nat, _, k, at in lay.pieces:
            up[:, nat : nat + 16] = gm[k, 0:R, at : at + 16]
        down = jnp.concatenate([gm[k, :, lay.up : lay.up + D] for k in range(lay.cuts)], axis=0)
    else:
        for k in range(FF // D):
            up[:, D * k : D * k + D] = gm[0, R * k : R * k + R, 0:D]
        down = gm[0, 0:Rd, D : 2 * D]
    step(2, slice(0, R), slice(0, FF), up[...], RATES[2], DECAY)
    put(2)
    step(3, slice(0, Rd), every, down, RATES[3], DECAY)
    put(3)
    g = jnp.concatenate([gq[k, 0:R, 128 * j : 128 * j + 128] for j in range(3) for k in range(3)], axis=1)
    step(0, slice(0, R), slice(0, 3 * D), g, RATES[0], DECAY)
    put(0)
    g = jnp.concatenate([gq[i % 3, R + i // 3 : R + i // 3 + 1] for i in range(R)], axis=0)
    step(1, slice(0, R), every, g, RATES[1], DECAY)
    put(1)
    me = lax.axis_index("dp") * (n // lax.axis_size("dp")) + lax.axis_index("fsdp")
    start = me * V
    row, lane = start // D, lax.rem(start, D)
    two = jnp.concatenate([small[pl.ds(row, 1), :], small[pl.ds(row + 1, 1), :]], axis=1)
    two = pltpu.roll(jnp.broadcast_to(two, (8, 2 * D)), 2 * D - lane, 1)
    step(4, slice(0, 1), slice(0, V), two[0:1, 0:V], VECTOR_RATE, 0.0)
    put(4)
    for c in stores + puts:
        c.wait()


def adam_call(n, small, squares, gq, gm, state, out, ig):
    vm = pl.BlockSpec(memory_space=pltpu.VMEM)
    hbm = pl.BlockSpec(memory_space=pl.ANY)
    S = jax.ShapeDtypeStruct
    V = pltpu.VMEM
    return pl.pallas_call(
        functools.partial(adam_kernel, n),
        out_shape=[S(out.shape, out.dtype), S(ig.shape, ig.dtype), S((1, 1), f32)] + [S(s.shape, f32) for s in state],
        in_specs=[vm] * 19 + [hbm] * 2,
        out_specs=[hbm] * 2 + [vm] + [hbm] * 15,
        scratch_shapes=[pltpu.SemaphoreType.DMA((31,)), V(out.shape, out.dtype), V(ig.shape, ig.dtype)]
        + [V((D // n, FF), f32)]
        + [V(s.shape, f32) for s in state],
        name="adam",
    )(small, squares, gq, gm, *state, out, ig)


def solution(mesh):
    n_dp, n_fs = mesh.shape["dp"], mesh.shape["fsdp"]
    X = n_fs // 2
    Y = X if n_dp % X == 0 else 1
    dims = (n_dp // Y, Y, X)
    n = n_dp * n_fs

    def per_device(x, dy, masks, *state):
        state = list(state)
        flat = [s.shape for s in state[12:15]]
        state[12:15] = [s.reshape(1, -1) for s in state[12:15]]
        out, ig, gq, gm, small, squares = layer_call(
            dims, x, dy, masks, state[0], state[3], state[6], state[9], state[12]
        )
        res = adam_call(n, small, squares, gq, gm, state, out, ig)
        new = list(res[3:])
        new[12:15] = [v.reshape(f) for v, f in zip(new[12:15], flat)]
        return (res[0], res[1], res[2].reshape(()), *new)

    rows = P(("dp", "fsdp"), None)
    line = P(("dp", "fsdp"))
    placed = (rows, rows, P(("dp", "fsdp"), None, None)) + (rows,) * 12 + (line,) * 3
    given = (rows, rows, P()) + (rows,) * 12 + (line,) * 3
    return jax.shard_map(per_device, mesh=mesh, in_specs=placed, out_specs=given, check_vma=False)
```

```python
import functools
import math

import jax
import jax.numpy as jnp
from jax import lax
from jax.experimental import pallas as pl
from jax.experimental.pallas import tpu as pltpu
from jax.sharding import PartitionSpec as P

D = 384
FF = 1536
HD = 64
STEP = 10
NORM_EPS = 1e-05
BETA1 = 0.9
BETA2 = 0.999
ADAM_EPS = 1e-08
DECAY = 0.05
RATES = (0.1, 0.5, 0.1, 0.05)
VECTOR_RATE = 1.0
TB = 512
TM = 1024
CH = 256

f32 = jnp.float32
bf16 = jnp.bfloat16
NN = (((1,), (0,)), ((), ()))
NT = (((1,), (1,)), ((), ()))
TN = (((0,), (0,)), ((), ()))
MESH = pl.DeviceIdType.MESH


def dot(a, b, dims=NN):
    return lax.dot_general(a, b, dims, preferred_element_type=f32)


def ln_parts(v):
    centered = v - jnp.mean(v, axis=-1, keepdims=True)
    variance = jnp.mean(centered * centered, axis=-1, keepdims=True)
    return centered, lax.rsqrt(variance + NORM_EPS)


def ln_back(grad, xhat, rstd, gain):
    t = grad * gain
    m1 = jnp.mean(t, axis=-1, keepdims=True)
    m2 = jnp.mean(t * xhat, axis=-1, keepdims=True)
    return rstd * (t - m1 - xhat * m2)


def gelu_parts(u):
    cdf = 0.5 + 0.5 * lax.erf(u * (2.0**-0.5))
    density = jnp.exp2(u * u * (-0.5 * math.log2(math.e))) * (1.0 / math.sqrt(2 * math.pi))
    return u * cdf, cdf + u * density


def lane_left():
    return lax.broadcasted_iota(jnp.int32, (64, 128), 1) < 64


def two_heads(m, left):
    zero = jnp.zeros_like(m)
    return jnp.concatenate([jnp.where(left, m, zero), jnp.where(left, zero, m)], axis=0)


def diagonal(r, left):
    return jnp.where(left, r[0:64], r[64:128])


def attention_forward(TA, i, g, mask, qkv, probs, mixed):
    left = lane_left()
    across = slice(128 * g, 128 * g + 128)
    clouds = TA // 64
    rows = [pl.ds(pl.multiple_of(i * TA + 64 * c, 64), 64) for c in range(clouds)]
    held = []
    for c, r in enumerate(rows):
        b = jnp.where(mask[i * clouds + c] == 1, 0.0, -1e30)
        q = qkv[r, D * g : D * g + 128] * jnp.asarray(0.125, bf16)
        k = qkv[r, D * g + 128 : D * g + 256]
        held.append(dot(k, two_heads(q, left), NT) + jnp.concatenate([b, b], axis=1))
    for c, r in enumerate(rows):
        s = held[c]
        e = jnp.exp(s - jnp.max(s, axis=0, keepdims=True))
        p = e * (1.0 / jnp.sum(e, axis=0, keepdims=True))
        probs[r, across] = p
        held[c] = p.astype(bf16)
    for c, r in enumerate(rows):
        v = qkv[r, D * g + 256 : D * g + 384]
        mixed[r, across] = diagonal(dot(held[c], v, TN), left).astype(bf16)


def attention_backward(TA, i, g, qkv, probs, dmix, dqkv):
    left = lane_left()
    across = slice(128 * g, 128 * g + 128)
    rows = [pl.ds(pl.multiple_of(i * TA + 64 * c, 64), 64) for c in range(TA // 64)]
    held = []
    for r in rows:
        v = qkv[r, D * g + 256 : D * g + 384]
        held.append(dot(v, two_heads(dmix[r, across], left), NT))
    for c, r in enumerate(rows):
        p, dp = probs[r, across], held[c]
        held[c] = (p * (dp - jnp.sum(p * dp, axis=0, keepdims=True))).astype(bf16)
    for ds, r in zip(held, rows):
        q = qkv[r, D * g : D * g + 128] * jnp.asarray(0.125, bf16)
        k = qkv[r, D * g + 128 : D * g + 256]
        dv = dot(probs[r, across].astype(bf16), two_heads(dmix[r, across], left))
        dk = dot(ds, two_heads(q, left))
        dq = diagonal(dot(ds, k, TN), left) * 0.125
        dqkv[r, D * g : D * g + 128] = dq.astype(bf16)
        dqkv[r, D * g + 128 : D * g + 256] = dk.astype(bf16)
        dqkv[r, D * g + 256 : D * g + 384] = dv.astype(bf16)


def pick_rows(devs, total, shift, step, k, block=None):
    rows = total // devs[2]
    shape = (16 * devs[1], total if block is None else D)
    out = lax.broadcasted_iota(jnp.int32, shape, 0)
    col = lax.broadcasted_iota(jnp.int32, shape, 1)
    if block is not None:
        col = col + D * block
    dev = out >> 4
    i = out - 16 * dev - shift
    ok = (i >= 0) & (i < rows // step) & (col == rows * (dev + devs[0]) + step * i + k)
    return jnp.where(ok, 1.0, 0.0).astype(bf16)


class Layout:
    def __init__(self, n):
        self.n, self.R, self.Rd = n, D // n, FF // n
        self.straight = self.Rd % 16 == 0
        self.cuts = self.Rd // 16 if self.straight else 1
        self.cw = FF // self.cuts
        self.up = self.cw if self.straight else D
        if self.straight:
            self.pieces = [
                (self.Rd * d + 16 * k, self.cw * k + 16 * d, k, 16 * d) for k in range(self.cuts) for d in range(n)
            ]
        self.blocks = ((16, D),) * 3 + ((16, self.up + D),) * self.cuts
        self.chunks = len(self.blocks)


def layer_kernel(dims, *refs):
    Z, Y, X = dims
    n = Z * Y * X * 2
    lay = Layout(n)
    R, Rd, NC, VEC = lay.R, lay.Rd, lay.chunks, lay.chunks
    MLP = list(range(3, NC))
    it = iter(refs)

    def take(count=None):
        return next(it) if count is None else [next(it) for _ in range(count)]

    x_hbm, dy_hbm, mask_hbm = take(3)
    own_hbm = take(5)
    out_hbm, ig_hbm, gq_hbm, gm_hbm, small_out, norm_out = take(6)
    own = take(5)
    wq_own, wp_own, wu_own, wd_own, vec_own = own
    gq_out, gm_out = take(2)
    x, dy, mask, a, qkv, probs, mixed, h1, dh1, c_all, z_all, du_all = take(12)
    bufs = take(NC + 1)
    wq, wp, wu, wd, vec, bu, vgrid, sel, tmp_q = take(9)
    stage = take(NC + 1)
    acc_p, dvec, dbu = take(3)
    r1, r2, r3 = take(NC), take(NC), take(NC)
    small, s1, s2, s3, sq, sq_in, far = take(7)
    local_sem, ag_send, ag_recv, rs_send, rs_recv, ar_send, ar_recv, sq_send, sq_recv, far_send, far_recv = take(11)
    outs = [gq_out.at[k] for k in range(3)] + [gm_out.at[k] for k in range(lay.cuts)]

    T = x.shape[0]
    V = vec_own.shape[1]
    TA = T if n <= 32 else T // 2
    dp = lax.axis_index("dp")
    fs = lax.axis_index("fsdp")
    z, y = dp // Y, lax.rem(dp, Y)
    xx, core = fs // 2, lax.rem(fs, 2)

    chips = [
        (lax.rem(z + k // (X * Y), Z), lax.rem(y + k // X % Y, Y), lax.rem(xx + k % X, X)) for k in range(1, Z * Y * X)
    ]
    chip_ids = [(c[0] * Y + c[1], c[2] * 2 + core) for c in chips]
    in_z = [k * X * Y - 1 for k in range(1, Z)]
    in_p = list(range(X * Y - 1))
    z_peers, z_ids = [chips[k] for k in in_z], [chip_ids[k] for k in in_z]
    p_peers, p_ids = [chips[k] for k in in_p], [chip_ids[k] for k in in_p]
    c_id = (dp, fs + 1 - 2 * core)
    P1, P2 = len(z_ids), len(p_ids)

    barrier = pltpu.get_barrier_semaphore()
    for dev in chip_ids + [c_id]:
        pl.semaphore_signal(barrier, inc=1, device_id=dev, device_id_type=MESH)

    own_loads = [pltpu.make_async_copy(a, b, local_sem.at[5 + k]) for k, (a, b) in enumerate(zip(own_hbm, own))]
    for c in own_loads:
        c.start()
    loads = [
        pltpu.make_async_copy(x_hbm, x, local_sem.at[0]),
        pltpu.make_async_copy(mask_hbm, mask, local_sem.at[1]),
        pltpu.make_async_copy(dy_hbm, dy, local_sem.at[2]),
    ]
    for c in loads:
        c.start()

    for t in stage:
        t[...] = jnp.zeros_like(t)
    for k in (0, 1, 4):
        own_loads[k].wait()
    for g in range(3):
        for j in range(3):
            stage[g][0:R, 128 * j : 128 * j + 128] = wq_own[:, D * j + 128 * g : D * j + 128 * g + 128]
    for i in range(R):
        stage[i % 3][R + i // 3 : R + i // 3 + 1] = wp_own[i : i + 1]
    stage[VEC][0:1, 0:V] = vec_own[...]
    for ch in (0, 1, 2, VEC):
        bufs[ch][z, y, xx, core] = stage[ch][...].astype(bf16)

    pl.semaphore_wait(barrier, len(chip_ids) + 1)

    def remote(src, dst, send, recv, dev):
        return pltpu.make_async_remote_copy(
            src_ref=src, dst_ref=dst, send_sem=send, recv_sem=recv, device_id=dev, device_id_type=MESH
        )

    def gather(ch, stage):
        g = bufs[ch]
        send, recv = ag_send.at[ch], ag_recv.at[ch]
        if stage == 0:
            own = g.at[z, y, xx, core]
            return [remote(own, own, send.at[j], recv.at[j], z_ids[j]) for j in range(P1)]
        if stage == 1:
            own = g.at[:, y, xx, core]
            return [remote(own, own, send.at[P1 + j], recv.at[P1 + j], p_ids[j]) for j in range(P2)]
        own = g.at[:, :, :, core]
        return [remote(own, own, send.at[P1 + P2], recv.at[P1 + P2], c_id)]

    def gather_step(ch, stage):
        if stage > 0:
            for c in gather(ch, stage - 1):
                c.wait()
        if stage < 3:
            for c in gather(ch, stage):
                c.start()

    def scatter(ch, stage):
        g = bufs[ch]
        send, recv = rs_send.at[ch], rs_recv.at[ch]
        if stage == 0:
            return [remote(g.at[:, :, :, 1 - core], r1[ch], send.at[P1 + P2], recv.at[P1 + P2], c_id)]
        if stage == 1:
            return [
                remote(g.at[:, p_peers[j][1], p_peers[j][2], core], r2[ch].at[j], send.at[P1 + j], recv.at[P1 + j], p_ids[j])
                for j in range(P2)
            ]
        return [
            remote(g.at[z_peers[j][0], y, xx, core], r3[ch].at[j], send.at[j], recv.at[j], z_ids[j]) for j in range(P1)
        ]

    def straight(ch):
        return [
            remote(bufs[ch].at[c[0], c[1], c[2], core], far.at[k], far_send.at[k], far_recv.at[k], chip_ids[k])
            for k, c in enumerate(chips)
        ]

    def straight_step(ch, stage):
        if stage == 0:
            for c in straight(ch):
                c.start()
        else:
            for c in straight(ch):
                c.wait()
            t = bufs[ch][z, y, xx, core].astype(f32)
            for k in range(len(chips)):
                t = t + far[k].astype(f32)
            outs[ch][...] = t

    def scatter_step(ch, stage):
        g = bufs[ch]
        if stage > 0:
            for c in scatter(ch, stage - 1):
                c.wait()
        if stage == 1:
            @pl.loop(0, Z)
            def _(zz):
                for yy in range(Y):
                    for cx in range(X):
                        t = g[zz, yy, cx, core].astype(f32) + r1[ch][zz, yy, cx].astype(f32)
                        g[zz, yy, cx, core] = t.astype(bf16)
        elif stage == 2:
            for zz in range(Z):
                t = g[zz, y, xx, core].astype(f32)
                for j in range(P2):
                    t = t + r2[ch][j, zz].astype(f32)
                g[zz, y, xx, core] = t.astype(bf16)
        elif stage == 3:
            t = g[z, y, xx, core].astype(f32)
            for j in range(P1):
                t = t + r3[ch][j].astype(f32)
            outs[ch][...] = t
        if ch == 2 and stage == 1:
            straight_step(ch, 0)
        elif stage < 3:
            for c in scatter(ch, stage):
                c.start()

    per_z = 2 * X * Y
    z_group = max(1, min(Z, 32 // per_z))
    count = z_group * per_z
    n_groups = Z // z_group
    SEL = {(0, 1, 0): 0, (R, 3, 0): 1, (R, 3, 1): 2, (R, 3, 2): 3}

    def pick(k, rows, shift, step, first, block=None):
        if n_groups == 1 and (shift, step, first) in SEL and rows == D:
            return sel[SEL[shift, step, first]]
        return pick_rows((k * count, count, n), rows, shift, step, first, block)

    def by_groups(f):
        if n_groups == 1:
            f(0)
        else:
            pl.loop(0, n_groups)(f)

    def unpack(into, cols, terms):
        def part(k):
            total = None
            for g, at, rows, shift, step, first, block in terms:
                flat = g[pl.ds(k * z_group, z_group), :, :, :, :, at].reshape(16 * count, at.stop - at.start)
                t = dot(pick(k, rows, shift, step, first, block), flat, TN)
                total = t if total is None else total + t
            if n_groups == 1:
                into[:, cols] = total.astype(bf16)
            else:
                into[:, cols] = (into[:, cols].astype(f32) + total).astype(bf16)

        if n_groups > 1:
            into[:, cols] = jnp.zeros((into.shape[0], cols.stop - cols.start), bf16)
        by_groups(part)

    def pack(g, at, terms, more=False):
        def one(k):
            total = None
            for source, rows, shift, step, first, block in terms:
                t = dot(pick(k, rows, shift, step, first, block), source[...])
                total = t if total is None else total + t
            where = pl.ds(k * z_group, z_group)
            total = total.reshape((z_group,) + g.shape[1:5] + (total.shape[1],))
            if more:
                total = total + g[where, :, :, :, :, at].astype(f32)
            g[where, :, :, :, :, at] = total.astype(bf16)

        by_groups(one)

    every = slice(0, D)

    for ch in (VEC, 0, 1, 2):
        gather_step(ch, 0)
    for k in (2, 3):
        own_loads[k].wait()
    if lay.straight:
        for nat, _, k, at in lay.pieces:
            stage[3 + k][0:R, at : at + 16] = wu_own[:, nat : nat + 16]
        for k in range(lay.cuts):
            stage[3 + k][:, lay.up : lay.up + D] = wd_own[16 * k : 16 * k + 16]
    else:
        for k in range(FF // D):
            stage[3][R * k : R * k + R, 0:D] = wu_own[:, D * k : D * k + D]
        stage[3][0:Rd, D : 2 * D] = wd_own[...]
    for ch in MLP:
        bufs[ch][z, y, xx, core] = stage[ch][...].astype(bf16)
        gather_step(ch, 0)
    if n_groups == 1:
        for (shift, step, first), k in SEL.items():
            sel[k] = pick_rows((0, n, n), D, shift, step, first)
    for r in (acc_p, dvec, dbu):
        r[...] = jnp.zeros_like(r)
    for c in loads:
        c.wait()

    @pl.loop(0, T // TB)
    def _(i):
        rows = pl.ds(pl.multiple_of(i * TB, TB), TB)
        centered, rstd = ln_parts(x[rows, :].astype(f32))
        h1[rows, :] = centered * rstd
        key = lax.broadcasted_iota(jnp.int32, (64, 64), 0)
        query = lax.broadcasted_iota(jnp.int32, (64, 64), 1)
        clouds = TB // 64
        for c in range(clouds):
            allowed = (key <= query) & ((mask[i * clouds + c].T == 1) | (key == query))
            mask[i * clouds + c] = jnp.where(allowed, 1, 0)

    for ch in (VEC, 0, 1, 2):
        gather_step(ch, 1)
    gather_step(MLP[0], 1)
    dvec[5:6] = jnp.sum(dy[...].astype(f32), axis=0, keepdims=True)
    gather_step(VEC, 2)
    gather_step(0, 2)
    gather_step(VEC, 3)
    for k in range(n_groups):
        row = lax.broadcasted_iota(jnp.int32, (count, 16 * count), 0)
        col = lax.broadcasted_iota(jnp.int32, (count, 16 * count), 1)
        pick_vec = jnp.where(col == 16 * row, 1.0, 0.0).astype(bf16)
        flat = bufs[VEC][k * z_group : (k + 1) * z_group].reshape(16 * count, 128)
        vgrid[k * count : (k + 1) * count] = dot(pick_vec, flat)
    for d in range(n):
        start, stop = V * d, V * d + V
        while start < stop:
            r0, l0 = start // D, start % D
            size = min(stop - start, D - l0)
            o = start - V * d
            vec[r0 : r0 + 1, l0 : l0 + size] = vgrid[d : d + 1, o : o + size]
            start += size

    def pair_forward(g):
        gather_step(g, 3)
        if g < 2:
            gather_step(g + 1, 2)
        if g + 1 < len(MLP):
            gather_step(MLP[g + 1], 1)
        mine = slice(D * g, D * g + D)
        unpack(wq, mine, [(bufs[g], every, D, 0, 1, 0, None)])

        @pl.loop(0, T // TA)
        def _(i):
            rows = pl.ds(pl.multiple_of(i * TA, TA), TA)
            if g == 0:
                av = (h1[rows, :] * vec[0:1] + vec[1:2]).astype(bf16)
                a[rows, :] = av
            else:
                av = a[rows, :]
            qkv[rows, mine] = dot(av, wq[:, mine]).astype(bf16)
            attention_forward(TA, i, g, mask, qkv, probs, mixed)

    for g in range(3):
        pair_forward(g)
    gather_step(MLP[0], 2)
    unpack(wp, every, [(bufs[k], every, D, R, 3, k, None) for k in range(3)])
    if lay.straight:
        for nat, place, _, _ in lay.pieces:
            r0, l0 = 6 + nat // D, nat % D
            bu[:, place : place + 16] = vec[r0 : r0 + 1, l0 : l0 + 16]
    else:
        for k in range(FF // D):
            bu[:, D * k : D * k + D] = vec[6 + k : 7 + k]

    @pl.loop(0, T // TB)
    def _(i):
        rows = pl.ds(pl.multiple_of(i * TB, TB), TB)
        h = x[rows, :].astype(f32) + (dot(mixed[rows, :], wp[...]) + vec[4:5])
        h1[rows, :] = h
        centered, rstd = ln_parts(h)
        c_all[rows, :] = (centered * rstd * vec[2:3] + vec[3:4]).astype(bf16)

    for k in range(lay.cuts):
        ch = 3 + k
        cut = slice(lay.cw * k, lay.cw * k + lay.cw)
        gather_step(ch, 3)
        if lay.straight:
            unpack(wu, cut, [(bufs[ch], slice(0, lay.up), D, 0, 1, 0, None)])
            wd[cut, :] = bufs[ch][:, :, :, :, :, lay.up : lay.up + D].reshape(lay.cw, D)
        else:
            for j in range(FF // D):
                unpack(wu, slice(D * j, D * j + D), [(bufs[ch], every, D, R * j, 1, 0, None)])
                unpack(wd.at[D * j : D * j + D], every, [(bufs[ch], slice(D, 2 * D), FF, 0, 1, 0, j)])

        @pl.loop(0, T // TM)
        def _(i):
            @pl.when(i == 1)
            def _():
                if k + 1 < lay.cuts:
                    gather_step(MLP[k + 1], 2)
                if k > 0:
                    scatter_step(ch - 1, 1)

            rows = pl.ds(pl.multiple_of(i * TM, TM), TM)
            c, dyv = c_all[rows, :], dy[rows, :]
            for start in range(cut.start, cut.stop, CH):
                ns = slice(start, start + CH)
                u = dot(c, wu[:, ns]) + bu[:, ns]
                dz = dot(dyv, wd[ns, :], NT)
                zv, slope = gelu_parts(u)
                z_all[rows, ns] = zv.astype(bf16)
                du = (dz * slope).astype(bf16)
                du_all[rows, ns] = du
                dbu[:, ns] += jnp.sum(du.astype(f32), axis=0, keepdims=True)

        if lay.straight:
            g = bufs[ch]
            down = dot(dy[...], z_all[:, cut], TN).astype(bf16).T
            g[:, :, :, :, :, lay.up : lay.up + D] = down.reshape(g.shape[:5] + (D,))
            pack(g, slice(0, lay.up), [(dot(c_all[...], du_all[:, cut], TN).astype(bf16), D, 0, 1, 0, None)])
        else:
            for j in range(FF // D):
                cols = slice(D * j, D * j + D)
                tmp_q[...] = dot(dy[...], z_all[:, cols], TN).astype(bf16).T
                pack(bufs[ch], slice(D, 2 * D), [(tmp_q, FF, 0, 1, 0, j)], j > 0)
                tmp_q[...] = dot(c_all[...], du_all[:, cols], TN).astype(bf16)
                pack(bufs[ch], every, [(tmp_q, D, R * j, 1, 0, None)], j > 0)
        scatter_step(ch, 0)

    dmix = mixed

    @pl.loop(0, 2)
    def _(i):
        rows = pl.ds(pl.multiple_of(i * TM, TM), TM)
        dc = dot(du_all[rows, :], wu[...], NT)
        centered, rstd = ln_parts(h1[rows, :])
        xhat = centered * rstd
        dvec[2:3] += jnp.sum(dc * xhat, axis=0, keepdims=True)
        dvec[3:4] += jnp.sum(dc, axis=0, keepdims=True)
        d1 = dy[rows, :].astype(f32) + ln_back(dc, xhat, rstd, vec[2:3])
        dh1[rows, :] = d1
        dr = d1.astype(bf16)
        dvec[4:5] += jnp.sum(dr.astype(f32), axis=0, keepdims=True)
        acc_p[...] += dot(mixed[rows, :], dr, TN)
        dmix[rows, :] = dot(dr, wp[...], NT).astype(bf16)

    scatter_step(MLP[-1], 1)
    if len(MLP) > 1:
        scatter_step(MLP[0], 2)
    wp[...] = acc_p[...].astype(bf16)

    small[0] = jnp.zeros((16, D), f32)
    small[0, 2:6] = dvec[2:6]
    if lay.straight:
        for nat, place, _, _ in lay.pieces:
            r0, l0 = 6 + nat // D, nat % D
            small[0, r0 : r0 + 1, l0 : l0 + 16] = dbu[:, place : place + 16]
    else:
        for k in range(FF // D):
            small[0, 6 + k : 7 + k] = dbu[:, D * k : D * k + D]
    received = (s1, s2, s3)

    def spread(stage):
        if stage == 0:
            return [remote(small.at[0], s1.at[j], ar_send.at[j], ar_recv.at[j], z_ids[j]) for j in range(P1)]
        if stage == 1:
            return [remote(small.at[1], s2.at[j], ar_send.at[P1 + j], ar_recv.at[P1 + j], p_ids[j]) for j in range(P2)]
        return [remote(small.at[2], s3.at[0], ar_send.at[P1 + P2], ar_recv.at[P1 + P2], c_id)]

    def spread_step(stage):
        if stage > 0:
            copies = spread(stage - 1)
            for c in copies:
                c.wait()
            t = small[stage - 1]
            for j in range(len(copies)):
                t = t + received[stage - 1][j]
            if stage < 3:
                small[stage] = t
            else:
                small_out[...] = t
        if stage < 3:
            for c in spread(stage):
                c.start()

    spread_step(0)

    dqkv = du_all

    def pair_backward(g):
        @pl.loop(0, 2)
        def _(i):
            attention_backward(T // 2, i, g, qkv, probs, dmix, dqkv)

        if g == 0 and len(MLP) > 2:
            scatter_step(MLP[1], 2)
        if g == 2:
            spread_step(1)
        if g > 0:
            scatter_step(g - 1, 1)
        if g == 1 and len(MLP) > 1:
            scatter_step(MLP[0], 3)
        if g == 2:
            scatter_step(MLP[-1], 2)
        tmp_q[...] = dot(a[...], dqkv[:, D * g : D * g + D], TN).astype(bf16)
        pack(bufs[g], every, [(tmp_q, D, 0, 1, 0, None), (wp, D, R, 3, g, None)])
        scatter_step(g, 0)

    for g in range(3):
        pair_backward(g)

    @pl.loop(0, T // TB)
    def _(i):
        @pl.when(i == 1)
        def _():
            scatter_step(2, 1)
            scatter_step(0, 2)

        @pl.when(i == 3)
        def _():
            if len(MLP) > 2:
                scatter_step(MLP[1], 3)
            scatter_step(1, 2)
            spread_step(2)

        rows = pl.ds(pl.multiple_of(i * TB, TB), TB)
        da = dot(dqkv[rows, 0 : 3 * D], wq[...], NT)
        centered, rstd = ln_parts(x[rows, :].astype(f32))
        xhat = centered * rstd
        dvec[0:1] += jnp.sum(da * xhat, axis=0, keepdims=True)
        dvec[1:2] += jnp.sum(da, axis=0, keepdims=True)
        dh1[rows, :] = dh1[rows, :] + ln_back(da, xhat, rstd, vec[0:1])

    put_ig = pltpu.make_async_copy(dh1, ig_hbm, local_sem.at[4])
    put_ig.start()

    @pl.loop(0, T // TB)
    def _(i):
        @pl.when(i == 1)
        def _():
            scatter_step(MLP[-1], 3)
            scatter_step(0, 3)

        rows = pl.ds(pl.multiple_of(i * TB, TB), TB)
        dy[rows, :] = (h1[rows, :] + (dot(z_all[rows, :], wd[...]) + vec[5:6])).astype(bf16)

    put_out = pltpu.make_async_copy(dy, out_hbm, local_sem.at[3])
    put_out.start()

    squares = jnp.zeros((1, 1), f32)
    spread_step(3)
    put_gm = pltpu.make_async_copy(gm_out, gm_hbm, local_sem.at[10])
    put_gm.start()
    for ch in MLP + [0, 1, 2]:
        if ch == 1:
            scatter_step(ch, 3)
        if ch == 2:
            straight_step(ch, 1)
            put_gq = pltpu.make_async_copy(gq_out, gq_hbm, local_sem.at[11])
            put_gq.start()
        t = outs[ch][...]
        squares = squares + jnp.sum(jnp.sum(t * t, axis=0, keepdims=True), axis=1, keepdims=True)
    for j in range(6):
        sq[0, j : j + 1] = dvec[j // 3 : j // 3 + 1, 128 * (j % 3) : 128 * (j % 3) + 128]
    sq[0, 6:8] = jnp.broadcast_to(squares, (2, 128))
    to_core = remote(sq.at[0], sq_in.at[len(chips)], sq_send.at[len(chips)], sq_recv.at[len(chips)], c_id)
    to_core.start()
    to_core.wait()
    sq[1] = sq[0] + sq_in[len(chips)]
    to_chips = [remote(sq.at[1], sq_in.at[j], sq_send.at[j], sq_recv.at[j], chip_ids[j]) for j in range(len(chips))]
    for c in to_chips:
        c.start()
    for c in to_chips:
        c.wait()
    total = sq[1]
    for j in range(len(chips)):
        total = total + sq_in[j]
    norm_out[...] = total
    for j in range(6):
        small_out[j // 3 : j // 3 + 1, 128 * (j % 3) : 128 * (j % 3) + 128] = total[j : j + 1]
    for c in (put_out, put_ig, put_gm, put_gq):
        c.wait()


def layer_call(dims, x, dy, masks, wq, wp, wu, wd, vec):
    Z, Y, X = dims
    n = Z * Y * X * 2
    lay = Layout(n)
    T = x.shape[0]
    S = jax.ShapeDtypeStruct
    V = pltpu.VMEM
    dma = pltpu.SemaphoreType.DMA
    vm = pl.BlockSpec(memory_space=pltpu.VMEM)
    hbm = pl.BlockSpec(memory_space=pl.ANY)
    P1, P2, chips = Z - 1, X * Y - 1, Z * Y * X - 1
    peers = P1 + P2 + 1
    blocks, NC = lay.blocks, lay.chunks
    one_group = n <= 32
    scratch = [V(w.shape, f32) for w in (wq, wp, wu, wd, vec)] + [V((3,) + blocks[0], f32), V((lay.cuts,) + blocks[3], f32)]
    scratch += [V((T, D), bf16), V((T, D), bf16), V(masks.shape, jnp.int32), V((T, D), bf16), V((T, 3 * D), bf16)]
    scratch += [V((T, D), f32), V((T, D), bf16), V((T, D), f32), V((T, D), f32), V((T, D), bf16)]
    scratch += [V((T, FF), bf16), V((T, FF), bf16)]
    scratch += [V((Z, Y, X, 2) + b, bf16) for b in blocks + ((16, 128),)]
    scratch += [V((D, 3 * D), bf16), V((D, D), bf16), V((D, FF), bf16), V((FF, D), bf16), V((16, D), f32), V((1, FF), f32)]
    scratch += [V((n, 128), f32), V((4, 16 * n, D) if one_group else (1, 16, 128), bf16), V((D, D), bf16)]
    scratch += [V(b, f32) for b in blocks + ((16, 128),)]
    scratch += [V((D, D), f32), V((8, D), f32), V((1, FF), f32)]
    scratch += [V((Z, Y, X) + b, bf16) for b in blocks]
    scratch += [V((P2, Z) + b, bf16) for b in blocks]
    scratch += [V((P1,) + b, bf16) for b in blocks]
    scratch += [V((3, 16, D), f32), V((P1, 16, D), f32), V((P2, 16, D), f32), V((1, 16, D), f32)]
    scratch += [V((2, 8, 128), f32), V((chips + 1, 8, 128), f32), V((chips,) + blocks[0], bf16)]
    scratch += [dma((20,))] + [dma((NC + 1, peers))] * 4 + [dma((peers,))] * 2 + [dma((chips + 1,))] * 2 + [dma((chips,))] * 2
    return pl.pallas_call(
        functools.partial(layer_kernel, dims),
        out_shape=[
            S((T, D), bf16), S((T, D), f32), S((3,) + blocks[0], f32), S((lay.cuts,) + blocks[3], f32),
            S((16, D), f32), S((8, 128), f32),
        ],
        in_specs=[hbm] * 8,
        out_specs=[hbm] * 4 + [vm] * 2,
        scratch_shapes=scratch,
        compiler_params=pltpu.CompilerParams(
            collective_id=0, has_side_effects=True, vmem_limit_bytes=62 * 1024 * 1024
        ),
        name="layer",
    )(x, dy, masks, wq, wp, wu, wd, vec)


def adam_step(w, m, r, g, rate, decay):
    m_new = BETA1 * m + (1.0 - BETA1) * g
    r_new = BETA2 * r + (1.0 - BETA2) * g * g
    m_hat = m_new / (1.0 - BETA1**STEP)
    r_hat = r_new / (1.0 - BETA2**STEP)
    return w - rate * (m_hat / (jnp.sqrt(r_hat) + ADAM_EPS) + decay * w), m_new, r_new


def adam_kernel(n, *refs):
    small_in, norm_in, gq_in, gm_in = refs[0:4]
    state_in = refs[4:19]
    out_in, ig_in = refs[19:21]
    out_ref, ig_ref, norm = refs[21:24]
    new_hbm = refs[24:39]
    sem, small, matrix_squares, gq, gm, out_v, ig_v, up = refs[39:47]
    state, new = refs[47:62], refs[62:77]
    lay = Layout(n)
    R, Rd, V = lay.R, lay.Rd, state[12].shape[1]
    T = out_v.shape[0]
    sems = iter(range(sem.shape[0]))

    def copy(a, b):
        return pltpu.make_async_copy(a, b, sem.at[next(sems)])

    first = [copy(a, b) for a, b in ((small_in, small), (norm_in, matrix_squares), (gm_in, gm), (gq_in, gq))]
    gets = [copy(a, b) for a, b in zip(state_in, state)]
    puts = [copy(a, b) for a, b in zip(new, new_hbm)]
    pieces = [pl.ds(k * (T // 4), T // 4) for k in range(4)]
    moves = [(a.at[r], b.at[r], c.at[r]) for r in pieces for a, b, c in ((ig_in, ig_v, ig_ref), (out_in, out_v, out_ref))]
    loads = [copy(a, b) for a, b, _ in moves]
    stores = [copy(b, c) for _, b, c in moves]
    order = (2, 3, 0, 1, 4)
    for c in first + [gets[3 * k + j] for k in order[:2] for j in range(3)] + loads[:2]:
        c.start()
    for c in [gets[3 * k + j] for k in order[2:] for j in range(3)] + loads[2:]:
        c.start()

    def pass_on(lo, hi):
        for c, d in zip(loads[lo:hi], stores[lo:hi]):
            c.wait()
            d.start()

    for c in first:
        c.wait()
    vecs = small[0:10]
    squares = jnp.sum(jnp.sum(vecs * vecs, axis=0, keepdims=True), axis=1, keepdims=True) + matrix_squares[6:7, 0:1]
    clip = jnp.sqrt(squares)
    norm[...] = clip
    factor = 1.0 / clip

    def step(k, g, rate, decay):
        for c in gets[3 * k : 3 * k + 3]:
            c.wait()
        w, m, r = (ref[...] for ref in state[3 * k : 3 * k + 3])
        for ref, value in zip(new[3 * k : 3 * k + 3], adam_step(w, m, r, g * factor, rate, decay)):
            ref[...] = value
        for c in puts[3 * k : 3 * k + 3]:
            c.start()

    if lay.straight:
        for nat, _, k, at in lay.pieces:
            up[:, nat : nat + 16] = gm[k, 0:R, at : at + 16]
        down = jnp.concatenate([gm[k, :, lay.up : lay.up + D] for k in range(lay.cuts)], axis=0)
    else:
        for k in range(FF // D):
            up[:, D * k : D * k + D] = gm[0, R * k : R * k + R, 0:D]
        down = gm[0, 0:Rd, D : 2 * D]
    pass_on(0, 2)
    step(2, up[...], RATES[2], DECAY)
    pass_on(2, 4)
    step(3, down, RATES[3], DECAY)
    pass_on(4, 6)
    g = jnp.concatenate([gq[k, 0:R, 128 * j : 128 * j + 128] for j in range(3) for k in range(3)], axis=1)
    step(0, g, RATES[0], DECAY)
    pass_on(6, 8)
    g = jnp.concatenate([gq[i % 3, R + i // 3 : R + i // 3 + 1] for i in range(R)], axis=0)
    step(1, g, RATES[1], DECAY)
    me = lax.axis_index("dp") * (n // lax.axis_size("dp")) + lax.axis_index("fsdp")
    start = me * V
    row, lane = start // D, lax.rem(start, D)
    two = jnp.concatenate([small[pl.ds(row, 1), :], small[pl.ds(row + 1, 1), :]], axis=1)
    two = pltpu.roll(jnp.broadcast_to(two, (8, 2 * D)), 2 * D - lane, 1)
    step(4, two[0:1, 0:V], VECTOR_RATE, 0.0)
    for c in stores + puts:
        c.wait()


def adam_call(n, small, squares, gq, gm, state, out, ig):
    vm = pl.BlockSpec(memory_space=pltpu.VMEM)
    hbm = pl.BlockSpec(memory_space=pl.ANY)
    S = jax.ShapeDtypeStruct
    V = pltpu.VMEM
    held = [V(v.shape, v.dtype) for v in (small, squares, gq, gm, out, ig)] + [V((D // n, FF), f32)]
    return pl.pallas_call(
        functools.partial(adam_kernel, n),
        out_shape=[S(out.shape, out.dtype), S(ig.shape, ig.dtype), S((1, 1), f32)] + [S(s.shape, f32) for s in state],
        in_specs=[hbm] * 21,
        out_specs=[hbm] * 2 + [vm] + [hbm] * 15,
        scratch_shapes=[pltpu.SemaphoreType.DMA((50,))] + held + [V(s.shape, f32) for s in state] * 2,
        compiler_params=pltpu.CompilerParams(vmem_limit_bytes=62 * 1024 * 1024),
        name="adam",
    )(small, squares, gq, gm, *state, out, ig)


def solution(mesh):
    n_dp, n_fs = mesh.shape["dp"], mesh.shape["fsdp"]
    X = n_fs // 2
    Y = X if n_dp % X == 0 else 1
    dims = (n_dp // Y, Y, X)
    n = n_dp * n_fs

    def per_device(x, dy, masks, *state):
        state = list(state)
        flat = [s.shape for s in state[12:15]]
        state[12:15] = [s.reshape(1, -1) for s in state[12:15]]
        out, ig, gq, gm, small, squares = layer_call(
            dims, x, dy, masks, state[0], state[3], state[6], state[9], state[12]
        )
        res = adam_call(n, small, squares, gq, gm, state, out, ig)
        new = list(res[3:])
        new[12:15] = [v.reshape(f) for v, f in zip(new[12:15], flat)]
        return (res[0], res[1], res[2].reshape(()), *new)

    rows = P(("dp", "fsdp"), None)
    line = P(("dp", "fsdp"))
    placed = (rows, rows, P(("dp", "fsdp"), None, None)) + (rows,) * 12 + (line,) * 3
    given = (rows, rows, P()) + (rows,) * 12 + (line,) * 3
    return jax.shard_map(per_device, mesh=mesh, in_specs=placed, out_specs=given, check_vma=False)
```

```python
import functools
import math

import jax
import jax.numpy as jnp
from jax import lax
from jax.experimental import pallas as pl
from jax.experimental.pallas import tpu as pltpu
from jax.sharding import PartitionSpec as P

D = 384
FF = 1536
HD = 64
STEP = 10
NORM_EPS = 1e-05
BETA1 = 0.9
BETA2 = 0.999
ADAM_EPS = 1e-08
DECAY = 0.05
RATES = (0.1, 0.5, 0.1, 0.05)
VECTOR_RATE = 1.0
TB = 512
TM = 1024
CH = 256

f32 = jnp.float32
bf16 = jnp.bfloat16
NN = (((1,), (0,)), ((), ()))
NT = (((1,), (1,)), ((), ()))
TN = (((0,), (0,)), ((), ()))
MESH = pl.DeviceIdType.MESH


def dot(a, b, dims=NN):
    return lax.dot_general(a, b, dims, preferred_element_type=f32)


def ln_parts(v):
    centered = v - jnp.mean(v, axis=-1, keepdims=True)
    variance = jnp.mean(centered * centered, axis=-1, keepdims=True)
    return centered, lax.rsqrt(variance + NORM_EPS)


def ln_back(grad, xhat, rstd, gain):
    t = grad * gain
    m1 = jnp.mean(t, axis=-1, keepdims=True)
    m2 = jnp.mean(t * xhat, axis=-1, keepdims=True)
    return rstd * (t - m1 - xhat * m2)


def gelu_parts(u):
    cdf = 0.5 + 0.5 * lax.erf(u * (2.0**-0.5))
    density = jnp.exp2(u * u * (-0.5 * math.log2(math.e))) * (1.0 / math.sqrt(2 * math.pi))
    return u * cdf, cdf + u * density


def lane_left():
    return lax.broadcasted_iota(jnp.int32, (64, 128), 1) < 64


def two_heads(m, left):
    zero = jnp.zeros_like(m)
    return jnp.concatenate([jnp.where(left, m, zero), jnp.where(left, zero, m)], axis=0)


def diagonal(r, left):
    return jnp.where(left, r[0:64], r[64:128])


def attention_forward(TA, i, g, mask, qkv, probs, mixed):
    left = lane_left()
    across = slice(128 * g, 128 * g + 128)
    clouds = TA // 64
    rows = [pl.ds(pl.multiple_of(i * TA + 64 * c, 64), 64) for c in range(clouds)]
    held = []
    for c, r in enumerate(rows):
        b = jnp.where(mask[i * clouds + c] == 1, 0.0, -1e30)
        q = qkv[r, D * g : D * g + 128] * jnp.asarray(0.125, bf16)
        k = qkv[r, D * g + 128 : D * g + 256]
        held.append(dot(k, two_heads(q, left), NT) + jnp.concatenate([b, b], axis=1))
    for c, r in enumerate(rows):
        s = held[c]
        e = jnp.exp(s - jnp.max(s, axis=0, keepdims=True))
        p = e * (1.0 / jnp.sum(e, axis=0, keepdims=True))
        probs[r, across] = p
        held[c] = p.astype(bf16)
    for c, r in enumerate(rows):
        v = qkv[r, D * g + 256 : D * g + 384]
        mixed[r, across] = diagonal(dot(held[c], v, TN), left).astype(bf16)


def attention_backward(TA, i, g, qkv, probs, dmix, dqkv):
    left = lane_left()
    across = slice(128 * g, 128 * g + 128)
    rows = [pl.ds(pl.multiple_of(i * TA + 64 * c, 64), 64) for c in range(TA // 64)]
    held = []
    for r in rows:
        v = qkv[r, D * g + 256 : D * g + 384]
        held.append(dot(v, two_heads(dmix[r, across], left), NT))
    for c, r in enumerate(rows):
        p, dp = probs[r, across], held[c]
        held[c] = (p * (dp - jnp.sum(p * dp, axis=0, keepdims=True))).astype(bf16)
    for ds, r in zip(held, rows):
        q = qkv[r, D * g : D * g + 128] * jnp.asarray(0.125, bf16)
        k = qkv[r, D * g + 128 : D * g + 256]
        dv = dot(probs[r, across].astype(bf16), two_heads(dmix[r, across], left))
        dk = dot(ds, two_heads(q, left))
        dq = diagonal(dot(ds, k, TN), left) * 0.125
        dqkv[r, D * g : D * g + 128] = dq.astype(bf16)
        dqkv[r, D * g + 128 : D * g + 256] = dk.astype(bf16)
        dqkv[r, D * g + 256 : D * g + 384] = dv.astype(bf16)


def pick_rows(devs, total, shift, step, k, block=None):
    rows = total // devs[2]
    shape = (16 * devs[1], total if block is None else D)
    out = lax.broadcasted_iota(jnp.int32, shape, 0)
    col = lax.broadcasted_iota(jnp.int32, shape, 1)
    if block is not None:
        col = col + D * block
    dev = out >> 4
    i = out - 16 * dev - shift
    ok = (i >= 0) & (i < rows // step) & (col == rows * (dev + devs[0]) + step * i + k)
    return jnp.where(ok, 1.0, 0.0).astype(bf16)


class Layout:
    def __init__(self, n):
        self.n, self.R, self.Rd = n, D // n, FF // n
        self.straight = self.Rd % 16 == 0
        self.cuts = self.Rd // 16 if self.straight else 1
        self.cw = FF // self.cuts
        self.up = self.cw if self.straight else D
        if self.straight:
            self.pieces = [
                (self.Rd * d + 16 * k, self.cw * k + 16 * d, k, 16 * d) for k in range(self.cuts) for d in range(n)
            ]
        self.blocks = ((16, D),) * 3 + ((16, self.up + D),) * self.cuts
        self.chunks = len(self.blocks)


def layer_kernel(dims, *refs):
    Z, Y, X = dims
    n = Z * Y * X * 2
    lay = Layout(n)
    R, Rd, NC, VEC = lay.R, lay.Rd, lay.chunks, lay.chunks
    MLP = list(range(3, NC))
    it = iter(refs)

    def take(count=None):
        return next(it) if count is None else [next(it) for _ in range(count)]

    x_hbm, dy_hbm, mask_hbm = take(3)
    own_hbm = take(5)
    out_hbm, ig_hbm, gq_hbm, gm_hbm, small_out, norm_out = take(6)
    own = take(5)
    wq_own, wp_own, wu_own, wd_own, vec_own = own
    gq_out, gm_out = take(2)
    x, dy, mask, a, qkv, probs, mixed, h1, dh1, c_all, z_all, du_all = take(12)
    bufs = take(NC + 1)
    wq, wp, wu, wd, vec, bu, vgrid, sel, tmp_q = take(9)
    stage = take(NC + 1)
    acc_p, dvec, dbu = take(3)
    r1, r2, r3 = take(NC), take(NC), take(NC)
    small, s1, s2, s3, sq, sq_in, far = take(7)
    local_sem, ag_send, ag_recv, rs_send, rs_recv, ar_send, ar_recv, sq_send, sq_recv, far_send, far_recv = take(11)
    outs = [gq_out.at[k] for k in range(3)] + [gm_out.at[k] for k in range(lay.cuts)]

    T = x.shape[0]
    V = vec_own.shape[1]
    TA = T if n <= 32 else T // 2
    dp = lax.axis_index("dp")
    fs = lax.axis_index("fsdp")
    z, y = dp // Y, lax.rem(dp, Y)
    xx, core = fs // 2, lax.rem(fs, 2)

    chips = [
        (lax.rem(z + k // (X * Y), Z), lax.rem(y + k // X % Y, Y), lax.rem(xx + k % X, X)) for k in range(1, Z * Y * X)
    ]
    chip_ids = [(c[0] * Y + c[1], c[2] * 2 + core) for c in chips]
    in_z = [k * X * Y - 1 for k in range(1, Z)]
    in_p = list(range(X * Y - 1))
    z_peers, z_ids = [chips[k] for k in in_z], [chip_ids[k] for k in in_z]
    p_peers, p_ids = [chips[k] for k in in_p], [chip_ids[k] for k in in_p]
    c_id = (dp, fs + 1 - 2 * core)
    P1, P2 = len(z_ids), len(p_ids)

    barrier = pltpu.get_barrier_semaphore()
    for dev in chip_ids + [c_id]:
        pl.semaphore_signal(barrier, inc=1, device_id=dev, device_id_type=MESH)

    own_loads = [pltpu.make_async_copy(a, b, local_sem.at[5 + k]) for k, (a, b) in enumerate(zip(own_hbm, own))]
    for c in own_loads:
        c.start()
    loads = [
        pltpu.make_async_copy(x_hbm, x, local_sem.at[0]),
        pltpu.make_async_copy(mask_hbm, mask, local_sem.at[1]),
        pltpu.make_async_copy(dy_hbm, dy, local_sem.at[2]),
    ]
    for c in loads:
        c.start()

    for t in stage:
        t[...] = jnp.zeros_like(t)
    for k in (0, 1, 4):
        own_loads[k].wait()
    for g in range(3):
        for j in range(3):
            stage[g][0:R, 128 * j : 128 * j + 128] = wq_own[:, D * j + 128 * g : D * j + 128 * g + 128]
    for i in range(R):
        stage[i % 3][R + i // 3 : R + i // 3 + 1] = wp_own[i : i + 1]
    stage[VEC][0:1, 0:V] = vec_own[...]
    for ch in (0, 1, 2, VEC):
        bufs[ch][z, y, xx, core] = stage[ch][...].astype(bf16)

    def remote(src, dst, send, recv, dev):
        return pltpu.make_async_remote_copy(
            src_ref=src, dst_ref=dst, send_sem=send, recv_sem=recv, device_id=dev, device_id_type=MESH
        )

    def gather(ch, stage):
        g = bufs[ch]
        send, recv = ag_send.at[ch], ag_recv.at[ch]
        if stage == 0:
            own = g.at[z, y, xx, core]
            return [remote(own, own, send.at[j], recv.at[j], z_ids[j]) for j in range(P1)]
        if stage == 1:
            own = g.at[:, y, xx, core]
            return [remote(own, own, send.at[P1 + j], recv.at[P1 + j], p_ids[j]) for j in range(P2)]
        own = g.at[:, :, :, core]
        return [remote(own, own, send.at[P1 + P2], recv.at[P1 + P2], c_id)]

    def gather_step(ch, stage):
        if stage > 0:
            for c in gather(ch, stage - 1):
                c.wait()
        if stage < 3:
            for c in gather(ch, stage):
                c.start()

    def scatter(ch, stage):
        g = bufs[ch]
        send, recv = rs_send.at[ch], rs_recv.at[ch]
        if stage == 0:
            return [remote(g.at[:, :, :, 1 - core], r1[ch], send.at[P1 + P2], recv.at[P1 + P2], c_id)]
        if stage == 1:
            return [
                remote(g.at[:, p_peers[j][1], p_peers[j][2], core], r2[ch].at[j], send.at[P1 + j], recv.at[P1 + j], p_ids[j])
                for j in range(P2)
            ]
        return [
            remote(g.at[z_peers[j][0], y, xx, core], r3[ch].at[j], send.at[j], recv.at[j], z_ids[j]) for j in range(P1)
        ]

    def straight(ch):
        return [
            remote(bufs[ch].at[c[0], c[1], c[2], core], far.at[k], far_send.at[k], far_recv.at[k], chip_ids[k])
            for k, c in enumerate(chips)
        ]

    def straight_step(ch, stage):
        if stage == 0:
            for c in straight(ch):
                c.start()
        else:
            for c in straight(ch):
                c.wait()
            t = bufs[ch][z, y, xx, core].astype(f32)
            for k in range(len(chips)):
                t = t + far[k].astype(f32)
            outs[ch][...] = t

    def scatter_step(ch, stage):
        g = bufs[ch]
        if stage > 0:
            for c in scatter(ch, stage - 1):
                c.wait()
        if stage == 1:
            @pl.loop(0, Z)
            def _(zz):
                for yy in range(Y):
                    for cx in range(X):
                        t = g[zz, yy, cx, core].astype(f32) + r1[ch][zz, yy, cx].astype(f32)
                        g[zz, yy, cx, core] = t.astype(bf16)
        elif stage == 2:
            for zz in range(Z):
                t = g[zz, y, xx, core].astype(f32)
                for j in range(P2):
                    t = t + r2[ch][j, zz].astype(f32)
                g[zz, y, xx, core] = t.astype(bf16)
        elif stage == 3:
            t = g[z, y, xx, core].astype(f32)
            for j in range(P1):
                t = t + r3[ch][j].astype(f32)
            outs[ch][...] = t
        if ch == 2 and stage == 1:
            straight_step(ch, 0)
        elif stage < 3:
            for c in scatter(ch, stage):
                c.start()

    per_z = 2 * X * Y
    z_group = max(1, min(Z, 32 // per_z))
    count = z_group * per_z
    n_groups = Z // z_group
    SEL = {(0, 1, 0): 0, (R, 3, 0): 1, (R, 3, 1): 2, (R, 3, 2): 3}

    def pick(k, rows, shift, step, first, block=None):
        if n_groups == 1 and (shift, step, first) in SEL and rows == D:
            return sel[SEL[shift, step, first]]
        return pick_rows((k * count, count, n), rows, shift, step, first, block)

    def by_groups(f):
        if n_groups == 1:
            f(0)
        else:
            pl.loop(0, n_groups)(f)

    def unpack(into, cols, terms):
        def part(k):
            total = None
            for g, at, rows, shift, step, first, block in terms:
                flat = g[pl.ds(k * z_group, z_group), :, :, :, :, at].reshape(16 * count, at.stop - at.start)
                t = dot(pick(k, rows, shift, step, first, block), flat, TN)
                total = t if total is None else total + t
            if n_groups == 1:
                into[:, cols] = total.astype(bf16)
            else:
                into[:, cols] = (into[:, cols].astype(f32) + total).astype(bf16)

        if n_groups > 1:
            into[:, cols] = jnp.zeros((into.shape[0], cols.stop - cols.start), bf16)
        by_groups(part)

    def pack(g, at, terms, more=False):
        def one(k):
            total = None
            for source, rows, shift, step, first, block in terms:
                t = dot(pick(k, rows, shift, step, first, block), source[...])
                total = t if total is None else total + t
            where = pl.ds(k * z_group, z_group)
            total = total.reshape((z_group,) + g.shape[1:5] + (total.shape[1],))
            if more:
                total = total + g[where, :, :, :, :, at].astype(f32)
            g[where, :, :, :, :, at] = total.astype(bf16)

        by_groups(one)

    every = slice(0, D)

    if n_groups == 1:
        for (shift, step, first), k in SEL.items():
            sel[k] = pick_rows((0, n, n), D, shift, step, first)
    for r in (acc_p, dvec, dbu):
        r[...] = jnp.zeros_like(r)
    for c in loads:
        c.wait()

    @pl.loop(0, T // TB)
    def _(i):
        rows = pl.ds(pl.multiple_of(i * TB, TB), TB)
        centered, rstd = ln_parts(x[rows, :].astype(f32))
        h1[rows, :] = centered * rstd
        key = lax.broadcasted_iota(jnp.int32, (64, 64), 0)
        query = lax.broadcasted_iota(jnp.int32, (64, 64), 1)
        clouds = TB // 64
        for c in range(clouds):
            allowed = (key <= query) & ((mask[i * clouds + c].T == 1) | (key == query))
            mask[i * clouds + c] = jnp.where(allowed, 1, 0)

    pl.semaphore_wait(barrier, len(chip_ids) + 1)

    for ch in (VEC, 0, 1, 2):
        gather_step(ch, 0)
    for k in (2, 3):
        own_loads[k].wait()
    if lay.straight:
        for nat, _, k, at in lay.pieces:
            stage[3 + k][0:R, at : at + 16] = wu_own[:, nat : nat + 16]
        for k in range(lay.cuts):
            stage[3 + k][:, lay.up : lay.up + D] = wd_own[16 * k : 16 * k + 16]
    else:
        for k in range(FF // D):
            stage[3][R * k : R * k + R, 0:D] = wu_own[:, D * k : D * k + D]
        stage[3][0:Rd, D : 2 * D] = wd_own[...]
    for ch in MLP:
        bufs[ch][z, y, xx, core] = stage[ch][...].astype(bf16)
        gather_step(ch, 0)
    for ch in (VEC, 0, 1, 2):
        gather_step(ch, 1)
    gather_step(MLP[0], 1)
    dvec[5:6] = jnp.sum(dy[...].astype(f32), axis=0, keepdims=True)
    gather_step(VEC, 2)
    gather_step(0, 2)
    gather_step(VEC, 3)
    for k in range(n_groups):
        row = lax.broadcasted_iota(jnp.int32, (count, 16 * count), 0)
        col = lax.broadcasted_iota(jnp.int32, (count, 16 * count), 1)
        pick_vec = jnp.where(col == 16 * row, 1.0, 0.0).astype(bf16)
        flat = bufs[VEC][k * z_group : (k + 1) * z_group].reshape(16 * count, 128)
        vgrid[k * count : (k + 1) * count] = dot(pick_vec, flat)
    for d in range(n):
        start, stop = V * d, V * d + V
        while start < stop:
            r0, l0 = start // D, start % D
            size = min(stop - start, D - l0)
            o = start - V * d
            vec[r0 : r0 + 1, l0 : l0 + size] = vgrid[d : d + 1, o : o + size]
            start += size

    if lay.straight:
        for nat, place, _, _ in lay.pieces:
            r0, l0 = 6 + nat // D, nat % D
            bu[:, place : place + 16] = vec[r0 : r0 + 1, l0 : l0 + 16]
    else:
        for k in range(FF // D):
            bu[:, D * k : D * k + D] = vec[6 + k : 7 + k]

    def pair_forward(g):
        gather_step(g, 3)
        if g < 2:
            gather_step(g + 1, 2)
        if g + 1 < len(MLP):
            gather_step(MLP[g + 1], 1)
        mine = slice(D * g, D * g + D)
        unpack(wq, mine, [(bufs[g], every, D, 0, 1, 0, None)])

        @pl.loop(0, T // TA)
        def _(i):
            rows = pl.ds(pl.multiple_of(i * TA, TA), TA)
            if g == 0:
                av = (h1[rows, :] * vec[0:1] + vec[1:2]).astype(bf16)
                a[rows, :] = av
            else:
                av = a[rows, :]
            qkv[rows, mine] = dot(av, wq[:, mine]).astype(bf16)
            attention_forward(TA, i, g, mask, qkv, probs, mixed)

    for g in range(3):
        pair_forward(g)
    gather_step(MLP[0], 2)
    unpack(wp, every, [(bufs[k], every, D, R, 3, k, None) for k in range(3)])
    @pl.loop(0, T // TB)
    def _(i):
        rows = pl.ds(pl.multiple_of(i * TB, TB), TB)
        h = x[rows, :].astype(f32) + (dot(mixed[rows, :], wp[...]) + vec[4:5])
        h1[rows, :] = h
        centered, rstd = ln_parts(h)
        c_all[rows, :] = (centered * rstd * vec[2:3] + vec[3:4]).astype(bf16)

    for k in range(lay.cuts):
        ch = 3 + k
        cut = slice(lay.cw * k, lay.cw * k + lay.cw)
        gather_step(ch, 3)
        if lay.straight:
            unpack(wu, cut, [(bufs[ch], slice(0, lay.up), D, 0, 1, 0, None)])
            wd[cut, :] = bufs[ch][:, :, :, :, :, lay.up : lay.up + D].reshape(lay.cw, D)
        else:
            for j in range(FF // D):
                unpack(wu, slice(D * j, D * j + D), [(bufs[ch], every, D, R * j, 1, 0, None)])
                unpack(wd.at[D * j : D * j + D], every, [(bufs[ch], slice(D, 2 * D), FF, 0, 1, 0, j)])

        @pl.loop(0, T // TM)
        def _(i):
            @pl.when(i == 1)
            def _():
                if k + 1 < lay.cuts:
                    gather_step(MLP[k + 1], 2)
                if k > 0:
                    scatter_step(ch - 1, 1)

            rows = pl.ds(pl.multiple_of(i * TM, TM), TM)
            c, dyv = c_all[rows, :], dy[rows, :]
            for start in range(cut.start, cut.stop, CH):
                ns = slice(start, start + CH)
                u = dot(c, wu[:, ns]) + bu[:, ns]
                dz = dot(dyv, wd[ns, :], NT)
                zv, slope = gelu_parts(u)
                z_all[rows, ns] = zv.astype(bf16)
                du = (dz * slope).astype(bf16)
                du_all[rows, ns] = du
                dbu[:, ns] += jnp.sum(du.astype(f32), axis=0, keepdims=True)

        if lay.straight:
            g = bufs[ch]
            down = dot(dy[...], z_all[:, cut], TN).astype(bf16).T
            g[:, :, :, :, :, lay.up : lay.up + D] = down.reshape(g.shape[:5] + (D,))
            pack(g, slice(0, lay.up), [(dot(c_all[...], du_all[:, cut], TN).astype(bf16), D, 0, 1, 0, None)])
        else:
            for j in range(FF // D):
                cols = slice(D * j, D * j + D)
                tmp_q[...] = dot(dy[...], z_all[:, cols], TN).astype(bf16).T
                pack(bufs[ch], slice(D, 2 * D), [(tmp_q, FF, 0, 1, 0, j)], j > 0)
                tmp_q[...] = dot(c_all[...], du_all[:, cols], TN).astype(bf16)
                pack(bufs[ch], every, [(tmp_q, D, R * j, 1, 0, None)], j > 0)
        scatter_step(ch, 0)

    dmix = mixed

    @pl.loop(0, 2)
    def _(i):
        rows = pl.ds(pl.multiple_of(i * TM, TM), TM)
        dc = dot(du_all[rows, :], wu[...], NT)
        centered, rstd = ln_parts(h1[rows, :])
        xhat = centered * rstd
        dvec[2:3] += jnp.sum(dc * xhat, axis=0, keepdims=True)
        dvec[3:4] += jnp.sum(dc, axis=0, keepdims=True)
        d1 = dy[rows, :].astype(f32) + ln_back(dc, xhat, rstd, vec[2:3])
        dh1[rows, :] = d1
        dr = d1.astype(bf16)
        dvec[4:5] += jnp.sum(dr.astype(f32), axis=0, keepdims=True)
        acc_p[...] += dot(mixed[rows, :], dr, TN)
        dmix[rows, :] = dot(dr, wp[...], NT).astype(bf16)

    scatter_step(MLP[-1], 1)
    if len(MLP) > 1:
        scatter_step(MLP[0], 2)
    wp[...] = acc_p[...].astype(bf16)

    small[0] = jnp.zeros((16, D), f32)
    small[0, 2:6] = dvec[2:6]
    if lay.straight:
        for nat, place, _, _ in lay.pieces:
            r0, l0 = 6 + nat // D, nat % D
            small[0, r0 : r0 + 1, l0 : l0 + 16] = dbu[:, place : place + 16]
    else:
        for k in range(FF // D):
            small[0, 6 + k : 7 + k] = dbu[:, D * k : D * k + D]
    received = (s1, s2, s3)

    def spread(stage):
        if stage == 0:
            return [remote(small.at[0], s1.at[j], ar_send.at[j], ar_recv.at[j], z_ids[j]) for j in range(P1)]
        if stage == 1:
            return [remote(small.at[1], s2.at[j], ar_send.at[P1 + j], ar_recv.at[P1 + j], p_ids[j]) for j in range(P2)]
        return [remote(small.at[2], s3.at[0], ar_send.at[P1 + P2], ar_recv.at[P1 + P2], c_id)]

    def spread_step(stage):
        if stage > 0:
            copies = spread(stage - 1)
            for c in copies:
                c.wait()
            t = small[stage - 1]
            for j in range(len(copies)):
                t = t + received[stage - 1][j]
            if stage < 3:
                small[stage] = t
            else:
                small_out[...] = t
        if stage < 3:
            for c in spread(stage):
                c.start()

    spread_step(0)

    dqkv = du_all

    def pair_backward(g):
        @pl.loop(0, 2)
        def _(i):
            attention_backward(T // 2, i, g, qkv, probs, dmix, dqkv)

        if g == 0 and len(MLP) > 2:
            scatter_step(MLP[1], 2)
        if g == 2:
            spread_step(1)
        if g > 0:
            scatter_step(g - 1, 1)
        if g == 1 and len(MLP) > 1:
            scatter_step(MLP[0], 3)
        if g == 2:
            scatter_step(MLP[-1], 2)
        tmp_q[...] = dot(a[...], dqkv[:, D * g : D * g + D], TN).astype(bf16)
        pack(bufs[g], every, [(tmp_q, D, 0, 1, 0, None), (wp, D, R, 3, g, None)])
        scatter_step(g, 0)

    for g in range(3):
        pair_backward(g)

    @pl.loop(0, T // TB)
    def _(i):
        @pl.when(i == 1)
        def _():
            scatter_step(2, 1)
            scatter_step(0, 2)

        @pl.when(i == 3)
        def _():
            if len(MLP) > 2:
                scatter_step(MLP[1], 3)
            scatter_step(1, 2)
            spread_step(2)

        rows = pl.ds(pl.multiple_of(i * TB, TB), TB)
        da = dot(dqkv[rows, 0 : 3 * D], wq[...], NT)
        centered, rstd = ln_parts(x[rows, :].astype(f32))
        xhat = centered * rstd
        dvec[0:1] += jnp.sum(da * xhat, axis=0, keepdims=True)
        dvec[1:2] += jnp.sum(da, axis=0, keepdims=True)
        dh1[rows, :] = dh1[rows, :] + ln_back(da, xhat, rstd, vec[0:1])

    put_ig = pltpu.make_async_copy(dh1, ig_hbm, local_sem.at[4])
    put_ig.start()

    @pl.loop(0, T // TB)
    def _(i):
        @pl.when(i == 1)
        def _():
            scatter_step(MLP[-1], 3)
            scatter_step(0, 3)

        rows = pl.ds(pl.multiple_of(i * TB, TB), TB)
        dy[rows, :] = (h1[rows, :] + (dot(z_all[rows, :], wd[...]) + vec[5:6])).astype(bf16)

    put_out = pltpu.make_async_copy(dy, out_hbm, local_sem.at[3])
    put_out.start()

    squares = jnp.zeros((1, 1), f32)
    spread_step(3)
    put_gm = pltpu.make_async_copy(gm_out, gm_hbm, local_sem.at[10])
    put_gm.start()
    for ch in MLP + [0, 1, 2]:
        if ch == 1:
            scatter_step(ch, 3)
        if ch == 2:
            straight_step(ch, 1)
            put_gq = pltpu.make_async_copy(gq_out, gq_hbm, local_sem.at[11])
            put_gq.start()
        t = outs[ch][...]
        squares = squares + jnp.sum(jnp.sum(t * t, axis=0, keepdims=True), axis=1, keepdims=True)
    for j in range(6):
        sq[0, j : j + 1] = dvec[j // 3 : j // 3 + 1, 128 * (j % 3) : 128 * (j % 3) + 128]
    sq[0, 6:8] = jnp.broadcast_to(squares, (2, 128))
    to_core = remote(sq.at[0], sq_in.at[len(chips)], sq_send.at[len(chips)], sq_recv.at[len(chips)], c_id)
    to_core.start()
    to_core.wait()
    sq[1] = sq[0] + sq_in[len(chips)]
    to_chips = [remote(sq.at[1], sq_in.at[j], sq_send.at[j], sq_recv.at[j], chip_ids[j]) for j in range(len(chips))]
    for c in to_chips:
        c.start()
    for c in to_chips:
        c.wait()
    total = sq[1]
    for j in range(len(chips)):
        total = total + sq_in[j]
    norm_out[...] = total
    for j in range(6):
        small_out[j // 3 : j // 3 + 1, 128 * (j % 3) : 128 * (j % 3) + 128] = total[j : j + 1]
    for c in (put_out, put_ig, put_gm, put_gq):
        c.wait()


def layer_call(dims, x, dy, masks, wq, wp, wu, wd, vec):
    Z, Y, X = dims
    n = Z * Y * X * 2
    lay = Layout(n)
    T = x.shape[0]
    S = jax.ShapeDtypeStruct
    V = pltpu.VMEM
    dma = pltpu.SemaphoreType.DMA
    vm = pl.BlockSpec(memory_space=pltpu.VMEM)
    hbm = pl.BlockSpec(memory_space=pl.ANY)
    P1, P2, chips = Z - 1, X * Y - 1, Z * Y * X - 1
    peers = P1 + P2 + 1
    blocks, NC = lay.blocks, lay.chunks
    one_group = n <= 32
    scratch = [V(w.shape, f32) for w in (wq, wp, wu, wd, vec)] + [V((3,) + blocks[0], f32), V((lay.cuts,) + blocks[3], f32)]
    scratch += [V((T, D), bf16), V((T, D), bf16), V(masks.shape, jnp.int32), V((T, D), bf16), V((T, 3 * D), bf16)]
    scratch += [V((T, D), f32), V((T, D), bf16), V((T, D), f32), V((T, D), f32), V((T, D), bf16)]
    scratch += [V((T, FF), bf16), V((T, FF), bf16)]
    scratch += [V((Z, Y, X, 2) + b, bf16) for b in blocks + ((16, 128),)]
    scratch += [V((D, 3 * D), bf16), V((D, D), bf16), V((D, FF), bf16), V((FF, D), bf16), V((16, D), f32), V((1, FF), f32)]
    scratch += [V((n, 128), f32), V((4, 16 * n, D) if one_group else (1, 16, 128), bf16), V((D, D), bf16)]
    scratch += [V(b, f32) for b in blocks + ((16, 128),)]
    scratch += [V((D, D), f32), V((8, D), f32), V((1, FF), f32)]
    scratch += [V((Z, Y, X) + b, bf16) for b in blocks]
    scratch += [V((P2, Z) + b, bf16) for b in blocks]
    scratch += [V((P1,) + b, bf16) for b in blocks]
    scratch += [V((3, 16, D), f32), V((P1, 16, D), f32), V((P2, 16, D), f32), V((1, 16, D), f32)]
    scratch += [V((2, 8, 128), f32), V((chips + 1, 8, 128), f32), V((chips,) + blocks[0], bf16)]
    scratch += [dma((20,))] + [dma((NC + 1, peers))] * 4 + [dma((peers,))] * 2 + [dma((chips + 1,))] * 2 + [dma((chips,))] * 2
    return pl.pallas_call(
        functools.partial(layer_kernel, dims),
        out_shape=[
            S((T, D), bf16), S((T, D), f32), S((3,) + blocks[0], f32), S((lay.cuts,) + blocks[3], f32),
            S((16, D), f32), S((8, 128), f32),
        ],
        in_specs=[hbm] * 8,
        out_specs=[hbm] * 4 + [vm] * 2,
        scratch_shapes=scratch,
        compiler_params=pltpu.CompilerParams(
            collective_id=0, has_side_effects=True, vmem_limit_bytes=62 * 1024 * 1024
        ),
        name="layer",
    )(x, dy, masks, wq, wp, wu, wd, vec)


def adam_step(w, m, r, g, rate, decay):
    m_new = BETA1 * m + (1.0 - BETA1) * g
    r_new = BETA2 * r + (1.0 - BETA2) * g * g
    m_hat = m_new / (1.0 - BETA1**STEP)
    r_hat = r_new / (1.0 - BETA2**STEP)
    return w - rate * (m_hat / (jnp.sqrt(r_hat) + ADAM_EPS) + decay * w), m_new, r_new


def adam_kernel(n, *refs):
    small_in, norm_in, gq_in, gm_in = refs[0:4]
    state_in = refs[4:19]
    out_in, ig_in = refs[19:21]
    out_ref, ig_ref, norm = refs[21:24]
    new_hbm = refs[24:39]
    sem, small, matrix_squares, gq, gm, out_v, ig_v, up = refs[39:47]
    state, new = refs[47:62], refs[62:77]
    lay = Layout(n)
    R, Rd, V = lay.R, lay.Rd, state[12].shape[1]
    T = out_v.shape[0]
    sems = iter(range(sem.shape[0]))

    def copy(a, b):
        return pltpu.make_async_copy(a, b, sem.at[next(sems)])

    first = [copy(a, b) for a, b in ((small_in, small), (norm_in, matrix_squares), (gm_in, gm), (gq_in, gq))]
    gets = [copy(a, b) for a, b in zip(state_in, state)]
    puts = [copy(a, b) for a, b in zip(new, new_hbm)]
    pieces = [pl.ds(k * (T // 2), T // 2) for k in range(2)]
    moves = [(a.at[r], b.at[r], c.at[r]) for r in pieces for a, b, c in ((ig_in, ig_v, ig_ref), (out_in, out_v, out_ref))]
    loads = [copy(a, b) for a, b, _ in moves]
    stores = [copy(b, c) for _, b, c in moves]
    order = (2, 3, 0, 1, 4)
    for c in first + [gets[3 * k + j] for k in order for j in range(3)] + loads:
        c.start()

    def pass_on(lo, hi):
        for c, d in zip(loads[lo:hi], stores[lo:hi]):
            c.wait()
            d.start()

    for c in first:
        c.wait()
    vecs = small[0:10]
    squares = jnp.sum(jnp.sum(vecs * vecs, axis=0, keepdims=True), axis=1, keepdims=True) + matrix_squares[6:7, 0:1]
    clip = jnp.sqrt(squares)
    norm[...] = clip
    factor = 1.0 / clip

    def step(k, g, rate, decay):
        for c in gets[3 * k : 3 * k + 3]:
            c.wait()
        w, m, r = (ref[...] for ref in state[3 * k : 3 * k + 3])
        for ref, value in zip(new[3 * k : 3 * k + 3], adam_step(w, m, r, g * factor, rate, decay)):
            ref[...] = value
        for c in puts[3 * k : 3 * k + 3]:
            c.start()

    if lay.straight:
        for nat, _, k, at in lay.pieces:
            up[:, nat : nat + 16] = gm[k, 0:R, at : at + 16]
        down = jnp.concatenate([gm[k, :, lay.up : lay.up + D] for k in range(lay.cuts)], axis=0)
    else:
        for k in range(FF // D):
            up[:, D * k : D * k + D] = gm[0, R * k : R * k + R, 0:D]
        down = gm[0, 0:Rd, D : 2 * D]
    pass_on(0, 1)
    step(2, up[...], RATES[2], DECAY)
    pass_on(1, 2)
    step(3, down, RATES[3], DECAY)
    pass_on(2, 3)
    g = jnp.concatenate([gq[k, 0:R, 128 * j : 128 * j + 128] for j in range(3) for k in range(3)], axis=1)
    step(0, g, RATES[0], DECAY)
    pass_on(3, 4)
    g = jnp.concatenate([gq[i % 3, R + i // 3 : R + i // 3 + 1] for i in range(R)], axis=0)
    step(1, g, RATES[1], DECAY)
    me = lax.axis_index("dp") * (n // lax.axis_size("dp")) + lax.axis_index("fsdp")
    start = me * V
    row, lane = start // D, lax.rem(start, D)
    two = jnp.concatenate([small[pl.ds(row, 1), :], small[pl.ds(row + 1, 1), :]], axis=1)
    two = pltpu.roll(jnp.broadcast_to(two, (8, 2 * D)), 2 * D - lane, 1)
    step(4, two[0:1, 0:V], VECTOR_RATE, 0.0)
    for c in stores + puts:
        c.wait()


def adam_call(n, small, squares, gq, gm, state, out, ig):
    vm = pl.BlockSpec(memory_space=pltpu.VMEM)
    hbm = pl.BlockSpec(memory_space=pl.ANY)
    S = jax.ShapeDtypeStruct
    V = pltpu.VMEM
    held = [V(v.shape, v.dtype) for v in (small, squares, gq, gm, out, ig)] + [V((D // n, FF), f32)]
    return pl.pallas_call(
        functools.partial(adam_kernel, n),
        out_shape=[S(out.shape, out.dtype), S(ig.shape, ig.dtype), S((1, 1), f32)] + [S(s.shape, f32) for s in state],
        in_specs=[hbm] * 21,
        out_specs=[hbm] * 2 + [vm] + [hbm] * 15,
        scratch_shapes=[pltpu.SemaphoreType.DMA((50,))] + held + [V(s.shape, f32) for s in state] * 2,
        compiler_params=pltpu.CompilerParams(vmem_limit_bytes=62 * 1024 * 1024),
        name="adam",
    )(small, squares, gq, gm, *state, out, ig)


def solution(mesh):
    n_dp, n_fs = mesh.shape["dp"], mesh.shape["fsdp"]
    X = n_fs // 2
    Y = X if n_dp % X == 0 else 1
    dims = (n_dp // Y, Y, X)
    n = n_dp * n_fs

    def per_device(x, dy, masks, *state):
        state = list(state)
        flat = [s.shape for s in state[12:15]]
        state[12:15] = [s.reshape(1, -1) for s in state[12:15]]
        out, ig, gq, gm, small, squares = layer_call(
            dims, x, dy, masks, state[0], state[3], state[6], state[9], state[12]
        )
        res = adam_call(n, small, squares, gq, gm, state, out, ig)
        new = list(res[3:])
        new[12:15] = [v.reshape(f) for v, f in zip(new[12:15], flat)]
        return (res[0], res[1], res[2].reshape(()), *new)

    rows = P(("dp", "fsdp"), None)
    line = P(("dp", "fsdp"))
    placed = (rows, rows, P(("dp", "fsdp"), None, None)) + (rows,) * 12 + (line,) * 3
    given = (rows, rows, P()) + (rows,) * 12 + (line,) * 3
    return jax.shard_map(per_device, mesh=mesh, in_specs=placed, out_specs=given, check_vma=False)
```
